256 devices in a mesh: dp: 2 (over z_lo), seq: 128 (over x, z_hi, y, core).
Axes of the slice: x: 4, y: 4, z: 8 (z_hi: 4, z_lo: 2; z = z_hi * 2 + z_lo), core: 2. Of those that a mesh axis runs over, the one named last changes fastest.
Arguments:
- inputs: bfloat16 [2, 131072, 1024], P('dp', 'seq'), may hold values from -24 to 24
- cotangent: bfloat16 [2, 131072, 1024], P('dp', 'seq'), may hold values from -0.29882812 to 0.29882812
- w_value: bfloat16 [1024, 1024], P('seq'), may hold values from -0.1875 to 0.1875
- right_factor: bfloat16 [256, 512, 512], P('seq'), may hold values from -0.25 to 0.25
- left_factor: bfloat16 [512, 256, 256], P('seq'), may hold values from -0.375 to 0.375
Outputs:
- mixed: bfloat16 [2, 131072, 1024], P('dp', 'seq')
- input_grad: bfloat16 [2, 131072, 1024], P('dp', 'seq')
- right_grad: float32 [256, 512, 512], P('seq')
- left_grad: float32 [512, 256, 256], P('seq')
- weight_grad: float32 [1024, 1024], P('seq')
The draws below stay inside these ranges and needn't reach their ends.
All inputs are finite; a program needn't handle non-finite values.
Results may differ from the reference program's by a relative error of at most 0.0064.
Values may be sent and summed in bfloat16 or wider, within the bound.
A program may use at most 128 MiB of HBM per device.

```python
import jax
import jax.numpy as jnp

D = 1024
OUTER = 256
INNER = 512
TOKENS = 131072
SEQS = 2


def strengthened(array, rng, source, target, blocks, factor):
    owner, partner = [(jnp.arange(array.shape[axis_at]) // (array.shape[axis_at] // blocks)).reshape([-1 if axis == axis_at else 1 for axis in range(array.ndim)]) for axis_at in (source, target)]
    chosen = jax.random.permutation(rng, blocks)[partner]
    strong = (owner == chosen) | (owner == (partner + blocks // 2) % blocks)
    return jnp.where(strong, factor * array, array)


def block_levels(stream_key, dims, cuts, smallest, high):
    level = 1.0
    for position, blocks in cuts:
        steps = jax.random.uniform(jax.random.fold_in(jax.random.fold_in(stream_key, 6), position), (blocks,), jnp.float32, smallest / len(cuts), high / len(cuts))
        level = level * jnp.repeat(jnp.exp(steps), dims[position] // blocks).reshape((-1,) + (1,) * (len(dims) - 1 - position))
    return level


def centred(key, extent, width, most, shards=(), held_as=jnp.bfloat16):
    result = width * jax.random.normal(key, extent, jnp.float32)
    if shards:
        result = result * block_levels(key, extent, shards, -0.22, 0.18)
    return jnp.clip(result, -most, most).astype(held_as)


def noise_with(key, shape, scale, limit, cuts, heavy, held_as=jnp.bfloat16):
    values = scale * jax.random.normal(key, shape, jnp.float32)
    if cuts:
        values = values * block_levels(key, shape, cuts, -0.22, 0.18)
    return jnp.clip(strengthened(values, jax.random.fold_in(key, 3), *heavy), -limit, limit).astype(held_as)


def setup_inputs(seed: int = 0) -> dict:
    key_list = jax.random.split(jax.random.key(seed), 6)
    return {
        "inputs": noise_with(key_list[0], (SEQS, TOKENS, D), 1.0, 24.0, ((0, 2), (1, 128)), (1, 2, 128, 5.5)),
        "cotangent": centred(key_list[1], (SEQS, TOKENS, D), 0.05, 0.29882812, ((0, 2), (1, 128))),
        "w_value": centred(key_list[2], (D, D), D ** -0.5, 0.1875, ((0, 128),)),
        "right_factor": centred(key_list[3], (OUTER, INNER, INNER), INNER ** -0.5, 0.25, ((0, 128),)),
        "left_factor": centred(key_list[4], (INNER, OUTER, OUTER), OUTER ** -0.5, 0.375, ((0, 128),)),
    }


def reference(inputs, cotangent, w_value, right_factor, left_factor):
    right32 = right_factor.astype(jnp.float32)
    left32 = left_factor.astype(jnp.float32)
    right_grad = jnp.zeros((OUTER, INNER, INNER), jnp.float32)
    left_grad = jnp.zeros((INNER, OUTER, OUTER), jnp.float32)
    weight_grad = jnp.zeros((D, D), jnp.float32)
    mixed_list = []
    input_list = []
    for index in range(SEQS):
        tokens = inputs[index]
        upstream = cotangent[index]
        value = jnp.dot(tokens, w_value, preferred_element_type=jnp.float32).astype(jnp.bfloat16)
        value_grid = value.reshape(OUTER, INNER, D).astype(jnp.float32)
        first = jnp.einsum('abc,acd->abd', right32, value_grid).astype(jnp.bfloat16)
        second = jnp.einsum('bxy,ybd->xbd', left32, first.astype(jnp.float32)).astype(jnp.bfloat16)
        second = second.reshape(TOKENS, D)
        mixed_list.append((tokens.astype(jnp.float32) * second.astype(jnp.float32)).astype(jnp.bfloat16))
        second_grad = (upstream.astype(jnp.float32) * tokens.astype(jnp.float32)).astype(jnp.bfloat16)
        second_grid = second_grad.reshape(OUTER, INNER, D).astype(jnp.float32)
        first_grad = jnp.einsum('bxy,xbd->ybd', left32, second_grid).astype(jnp.bfloat16)
        left_grad = left_grad + jnp.einsum('xbd,ybd->bxy', second_grid, first.astype(jnp.float32))
        first_grid = first_grad.astype(jnp.float32)
        value_grad = jnp.einsum('abc,abd->acd', right32, first_grid).astype(jnp.bfloat16)
        right_grad = right_grad + jnp.einsum('abd,acd->abc', first_grid, value_grid)
        value_grad = value_grad.reshape(TOKENS, D)
        weight_grad = weight_grad + jnp.dot(tokens.T, value_grad, preferred_element_type=jnp.float32)
        back = jnp.dot(value_grad, w_value.T, preferred_element_type=jnp.float32)
        input_list.append((upstream.astype(jnp.float32) * second.astype(jnp.float32) + back).astype(jnp.bfloat16))
    return (jnp.stack(mixed_list), jnp.stack(input_list), right_grad, left_grad, weight_grad)
```

```python
import jax
import jax.numpy as jnp
from jax import lax
from jax.experimental import pallas as pl
from jax.experimental.pallas import tpu as pltpu
from jax.sharding import PartitionSpec as P

MESH = pl.DeviceIdType.MESH
F32 = jnp.float32
BF16 = jnp.bfloat16
N = 128
X4, Z4, Y4, C2 = 4, 4, 4, 2


def seq_of(x, z, y, c):
    return ((x * Z4 + z) * Y4 + y) * C2 + c


def dot(a, b, ca=1, cb=0):
    return lax.dot_general(a, b, (((ca,), (cb,)), ((), ())), preferred_element_type=F32)


def pack(x):
    return jnp.concatenate([x[:, :, :256], x[:, :, 256:]], axis=1).astype(BF16)


def unpack(w):
    w = w.astype(F32)
    return jnp.concatenate([w[:, :8, :], w[:, 8:, :]], axis=2)


def low_rows(shape):
    return lax.broadcasted_iota(jnp.int32, shape, 1) < 4


def interleave(t0, t1):
    low = low_rows(t0.shape)
    even = jnp.where(low, t0, pltpu.roll(t1, 4, 1))
    odd = jnp.where(low, pltpu.roll(t0, 4, 1), t1)
    return jnp.stack([even, odd], axis=1).reshape(2 * t0.shape[0], 8, t0.shape[2])


def deinterleave(w):
    pair = w.reshape(w.shape[0] // 2, 2, 8, w.shape[2])
    even, odd = pair[:, 0], pair[:, 1]
    low = low_rows(even.shape)
    return jnp.where(low, even, pltpu.roll(odd, 4, 1)), jnp.where(low, pltpu.roll(even, 4, 1), odd)


def loop(count, step):
    def run(i, carry):
        step(i)
        return carry

    lax.fori_loop(0, count, run, 0)


def at(i, size):
    return pl.ds(pl.multiple_of(i * size, size), size)


def mixer(
    x_ref, u_ref, w_ref, r_ref, l_ref,
    mixed_hbm, igrad_hbm, rgrad_hbm, lgrad_hbm, wgrad_ref,
    s1, r1, s2, r2, s3, r3, s4, r4,
    wall, wm, m_ref, mt_ref, t_ref, g_ref, f_ref, v_ref, fg_ref, vg_ref,
    lg_big, lg_mid, lg_own, lg_other, lg_sum, rg_own, rg_other, rg_sum,
    core_in, plane_out, plane_in, z_out, z_in, back_ref, mixed_ref, igrad_ref,
    send_sem, recv_sem, own_sem, w_sem, x_sem, out_sem,
):
    me = lax.axis_index("seq")
    dp = lax.axis_index("dp")
    x = lax.div(me, 32)
    z = lax.rem(lax.div(me, 8), 4)
    y = lax.rem(lax.div(me, 2), 4)
    c = lax.rem(me, 2)

    def remote(src, dst, send, recv, target, group=None):
        return pltpu.make_async_remote_copy(
            src_ref=src, dst_ref=dst, send_sem=send, recv_sem=recv,
            device_id=(dp if group is None else group, target), device_id_type=MESH,
        )

    def settle(ref, sem):
        pltpu.make_async_copy(ref, ref, sem).wait()

    def exchange(i, src, dst):
        pltpu.make_async_copy(src.at[me], dst.at[me], own_sem.at[i]).start()

        def send(k):
            d = lax.rem(me + k + 1, N)
            remote(src.at[d], dst.at[me], send_sem.at[i], recv_sem.at[i], d).start()

        loop(N - 1, send)

    def arrived(i, src, dst):
        pltpu.make_async_copy(src.at[me], dst.at[me], own_sem.at[i]).wait()
        settle(dst.at[pl.ds(0, N - 1)], recv_sem.at[i])

    def sent(i, src):
        settle(src.at[pl.ds(0, N - 1)], send_sem.at[i])

    for m in range(2):
        rows = w_ref[:, 512 * m : 512 * m + 512].astype(F32).reshape(1, 8, 512)
        wall[x, z, y, c, :, 256 * m : 256 * m + 256] = pack(rows).reshape(16, 256)

    def spread(phase, block, targets):
        for t in targets:
            remote(block, block, w_sem.at[2 * phase], w_sem.at[2 * phase + 1], t).start()

    def spread_done(phase, like):
        settle(like, w_sem.at[2 * phase + 1])
        settle(like, w_sem.at[2 * phase])

    spread(0, wall.at[x, z, y, c], [seq_of(x, lax.rem(z + i, 4), y, c) for i in (1, 2, 3)])

    def second_grad(i):
        a0, a1 = at(i, 32), pl.ds(pl.multiple_of(512 + i * 32, 32), 32)
        for m in range(2):
            cols = slice(512 * m, 512 * m + 512)
            t0 = x_ref[a0, cols].astype(F32) * u_ref[a0, cols].astype(F32)
            t1 = x_ref[a1, cols].astype(F32) * u_ref[a1, cols].astype(F32)
            both = interleave(t0.reshape(4, 8, 512), t1.reshape(4, 8, 512))
            s1[at(i, 8), :, 256 * m : 256 * m + 256] = pack(both)

    loop(16, second_grad)
    exchange(0, s1, r1)

    def widen(b):
        select = (
            lax.broadcasted_iota(jnp.int32, (256, 1024), 1)
            == 4 * lax.broadcasted_iota(jnp.int32, (256, 1024), 0) + b
        ).astype(F32).astype(BF16)
        return select

    def place(i):
        row = lax.broadcasted_iota(jnp.int32, (256, 1024), 0) + i * 256
        col = lax.broadcasted_iota(jnp.int32, (256, 1024), 1)
        return (4 * lax.rem(col, 256) + lax.div(col, 256) == row).astype(F32).astype(BF16)

    def build(transposed, out):
        def wide(b):
            t_ref[at(b, 256), :] = dot(l_ref[b], widen(b), ca=0 if transposed else 1).astype(BF16)

        loop(4, wide)

        def rows(i):
            out[at(i, 256), :] = dot(place(i), t_ref[...]).astype(BF16)

        loop(4, rows)

    spread_done(0, wall.at[0, pl.ds(0, 3), 0, 0])
    spread(1, wall.at[x, :, y, c], [seq_of(lax.rem(x + i, 4), z, y, c) for i in (1, 2, 3)])
    build(True, mt_ref)
    spread_done(1, wall.at[pl.ds(0, 3), :, 0, 0])
    spread(2, wall.at[:, :, y, c], [seq_of(x, z, lax.rem(y + i, 4), c) for i in (1, 2, 3)])
    build(False, m_ref)
    spread_done(2, wall.at[:, :, pl.ds(0, 3), 0])
    spread(3, wall.at[:, :, :, c], [seq_of(x, z, y, 1 - c)])
    spread_done(3, wall.at[:, :, :, 0])

    def unpack_weight(i):
        for m in range(2):
            part = wall[i, :, :, :, :, 256 * m : 256 * m + 256].reshape(32, 16, 256)
            wm[at(i, 256), 512 * m : 512 * m + 512] = unpack(part).reshape(256, 512).astype(BF16)

    loop(4, unpack_weight)

    def value(i):
        v_ref[at(i, 256), :] = dot(x_ref[at(i, 256), :], wm[...]).astype(BF16)

    loop(4, value)

    def first(i):
        for m in range(2):
            cols = slice(512 * m, 512 * m + 512)
            t0 = dot(r_ref[0, at(i, 256), :], v_ref[0:512, cols])
            t1 = dot(r_ref[1, at(i, 256), :], v_ref[512:1024, cols])
            both = interleave(t0.reshape(32, 8, 512), t1.reshape(32, 8, 512))
            s2[at(i, 64), :, 256 * m : 256 * m + 256] = pack(both)

    loop(2, first)
    exchange(1, s2, r2)

    def unpack_all(src, dst):
        def step(i):
            for m in range(2):
                part = src[at(i, 16), :, 256 * m : 256 * m + 256]
                dst[at(i, 128), 512 * m : 512 * m + 512] = unpack(part).reshape(128, 512).astype(BF16)

        loop(8, step)

    def columns_product(big, cols_ref, out):
        def step(i):
            for m in range(2):
                t = dot(big[at(i, 256), :], cols_ref[:, 512 * m : 512 * m + 512])
                out[at(i, 32), :, 256 * m : 256 * m + 256] = pack(t.reshape(32, 8, 512))

        loop(4, step)

    arrived(0, s1, r1)
    unpack_all(r1, g_ref)
    columns_product(mt_ref, g_ref, s3)
    exchange(2, s3, r3)

    arrived(1, s2, r2)
    unpack_all(r2, f_ref)
    columns_product(m_ref, f_ref, s4)
    exchange(3, s4, r4)

    def left_all(i):
        rows = dot(g_ref[at(i, 256), :], f_ref[...], cb=1)
        row = lax.broadcasted_iota(jnp.int32, (256, 1024), 0)
        col = lax.broadcasted_iota(jnp.int32, (256, 1024), 1)
        lg_big[at(i, 256), :] = jnp.where(lax.rem(row, 4) == lax.rem(col, 4), rows, 0.0).astype(BF16)

    loop(4, left_all)

    def left_narrow(i):
        c_row = lax.broadcasted_iota(jnp.int32, (1024, 256), 0)
        c_col = lax.broadcasted_iota(jnp.int32, (1024, 256), 1)
        narrow = (lax.div(c_row, 4) == c_col).astype(F32).astype(BF16)
        lg_mid[at(i, 256), :] = dot(lg_big[at(i, 256), :], narrow).astype(BF16)

    loop(4, left_narrow)

    def left_place(b):
        row = lax.broadcasted_iota(jnp.int32, (256, 1024), 0)
        col = lax.broadcasted_iota(jnp.int32, (256, 1024), 1)
        take = (4 * row + b == col).astype(F32).astype(BF16)
        lg_own[b] = dot(take, lg_mid[...]).astype(BF16)

    loop(4, left_place)
    left_swap = remote(lg_own, lg_other, x_sem.at[0], x_sem.at[1], me, 1 - dp)
    left_swap.start()

    arrived(2, s3, r3)

    def first_grad(i):
        for m in range(2):
            t0, t1 = deinterleave(unpack(r3[at(i, 16), :, 256 * m : 256 * m + 256]))
            cols = slice(512 * m, 512 * m + 512)
            fg_ref[at(i, 64), cols] = t0.reshape(64, 512).astype(BF16)
            fg_ref[pl.ds(pl.multiple_of(512 + i * 64, 64), 64), cols] = t1.reshape(64, 512).astype(BF16)

    loop(8, first_grad)

    def right_part(i):
        rg_own[i] = dot(fg_ref[at(i, 512), :], v_ref[at(i, 512), :], cb=1).astype(BF16)

    loop(2, right_part)
    right_swap = remote(rg_own, rg_other, x_sem.at[2], x_sem.at[3], me, 1 - dp)
    right_swap.start()

    def value_grad(i):
        vg_ref[at(i, 512), :] = dot(r_ref[i], fg_ref[at(i, 512), :], ca=0).astype(BF16)

    loop(2, value_grad)

    def weight_part(i):
        for m in range(2):
            t = dot(x_ref[:, at(i, 256)], vg_ref[:, 512 * m : 512 * m + 512], ca=0)
            wall[i, :, :, :, :, 256 * m : 256 * m + 256] = pack(t.reshape(32, 8, 512)).reshape(4, 4, 2, 16, 256)

    loop(4, weight_part)
    to_core = remote(wall.at[:, :, :, 1 - c], core_in, x_sem.at[4], x_sem.at[5], seq_of(x, z, y, 1 - c))
    to_core.start()

    def back(i):
        back_ref[at(i, 256), :] = dot(vg_ref[at(i, 256), :], wm[...], cb=1)

    loop(2, back)
    to_core.wait()

    def add_core(i):
        mine = wall[i, :, :, c].astype(F32)
        plane_out[i] = (mine + core_in[i].astype(F32)).astype(BF16)

    loop(4, add_core)
    keep = pltpu.make_async_copy(plane_out.at[x, :, y], plane_in.at[x, y], own_sem.at[4])
    keep.start()
    for i in range(1, 16):
        tx, ty = lax.rem(x + i // 4, 4), lax.rem(y + i % 4, 4)
        remote(plane_out.at[tx, :, ty], plane_in.at[x, y], x_sem.at[6], x_sem.at[7], seq_of(tx, z, ty, c)).start()

    loop(2, lambda i: back(i + 2))
    keep.wait()
    settle(s1.at[pl.ds(0, 60)], x_sem.at[7])
    settle(s1.at[pl.ds(0, 60)], x_sem.at[6])

    def add_plane(i):
        total = jnp.zeros((16, 512), F32)
        for j in range(16):
            total = total + plane_in[j // 4, j % 4, i].astype(F32)
        z_out[i] = total.astype(BF16)

    loop(4, add_plane)
    zz = z * 2 + dp
    keep = pltpu.make_async_copy(z_out.at[z], z_in.at[zz], own_sem.at[5])
    keep.start()
    for i in range(1, 8):
        tz = lax.rem(zz + i, 8)
        th = lax.div(tz, 2)
        remote(z_out.at[th], z_in.at[zz], x_sem.at[8], x_sem.at[9], seq_of(x, th, y, c), lax.rem(tz, 2)).start()

    left_swap.wait()

    def left_sum(b):
        lg_sum[b] = lg_own[b].astype(F32) + lg_other[b].astype(F32)

    loop(4, left_sum)
    left_out = pltpu.make_async_copy(lg_sum, lgrad_hbm, out_sem.at[0])
    left_out.start()

    right_swap.wait()

    def right_sum(i):
        for a in range(2):
            rg_sum[a, at(i, 128), :] = rg_own[a, at(i, 128), :].astype(F32) + rg_other[a, at(i, 128), :].astype(F32)

    loop(4, right_sum)
    right_out = pltpu.make_async_copy(rg_sum, rgrad_hbm, out_sem.at[1])
    right_out.start()

    arrived(3, s4, r4)

    def finish(i):
        for m in range(2):
            cols = slice(512 * m, 512 * m + 512)
            parts = deinterleave(unpack(r4[at(i, 16), :, 256 * m : 256 * m + 256]))
            for a in range(2):
                rows = pl.ds(pl.multiple_of(512 * a + i * 64, 64), 64)
                second = parts[a].reshape(64, 512)
                mixed_ref[rows, cols] = (x_ref[rows, cols].astype(F32) * second).astype(BF16)
                igrad_ref[rows, cols] = (u_ref[rows, cols].astype(F32) * second + back_ref[rows, cols]).astype(BF16)

    loop(8, finish)
    mixed_out = pltpu.make_async_copy(mixed_ref, mixed_hbm, out_sem.at[2])
    mixed_out.start()
    igrad_out = pltpu.make_async_copy(igrad_ref, igrad_hbm, out_sem.at[3])
    igrad_out.start()

    keep.wait()
    settle(z_in.at[pl.ds(0, 7)], x_sem.at[9])
    settle(z_in.at[pl.ds(0, 7)], x_sem.at[8])
    total = jnp.zeros((16, 512), F32)
    for j in range(8):
        total = total + z_in[j].astype(F32)
    for m in range(2):
        for h in range(2):
            wgrad_ref[:, 512 * m + 256 * h : 512 * m + 256 * h + 256] = total[8 * h : 8 * h + 8, 256 * m : 256 * m + 256]

    sent(0, s1)
    sent(1, s2)
    sent(2, s3)
    sent(3, s4)
    left_out.wait()
    right_out.wait()
    mixed_out.wait()
    igrad_out.wait()


def body(inputs, cotangent, w_value, right_factor, left_factor):
    vmem = pl.BlockSpec(memory_space=pltpu.VMEM)
    hbm = pl.BlockSpec(memory_space=pl.ANY)

    def scratch(*shape, dtype=BF16):
        return pltpu.VMEM(shape, dtype)

    square = scratch(1024, 1024)
    wire = scratch(N, 16, 512)
    mixed, igrad, rgrad, lgrad, wgrad = pl.pallas_call(
        mixer,
        name="mixer",
        out_shape=(
            jax.ShapeDtypeStruct((1024, 1024), BF16),
            jax.ShapeDtypeStruct((1024, 1024), BF16),
            jax.ShapeDtypeStruct((2, 512, 512), F32),
            jax.ShapeDtypeStruct((4, 256, 256), F32),
            jax.ShapeDtypeStruct((8, 1024), F32),
        ),
        in_specs=[vmem] * 5,
        out_specs=(hbm, hbm, hbm, hbm, vmem),
        scratch_shapes=[wire] * 8
        + [scratch(4, 4, 4, 2, 16, 512)]
        + [square] * 9
        + [square, scratch(1024, 256), scratch(4, 256, 256), scratch(4, 256, 256), scratch(4, 256, 256, dtype=F32)]
        + [scratch(2, 512, 512), scratch(2, 512, 512), scratch(2, 512, 512, dtype=F32)]
        + [scratch(4, 4, 4, 16, 512)] * 3
        + [scratch(4, 16, 512), scratch(8, 16, 512), scratch(1024, 1024, dtype=F32), square, square]
        + [pltpu.SemaphoreType.DMA((4,))] * 2
        + [pltpu.SemaphoreType.DMA((6,)), pltpu.SemaphoreType.DMA((8,)), pltpu.SemaphoreType.DMA((10,)), pltpu.SemaphoreType.DMA((4,))],
        compiler_params=pltpu.CompilerParams(has_side_effects=True, vmem_limit_bytes=62 << 20),
        cost_estimate=pl.CostEstimate(flops=26_000_000_000, bytes_accessed=14_000_000, transcendentals=0),
    )(inputs.reshape(1024, 1024), cotangent.reshape(1024, 1024), w_value, right_factor, left_factor)
    shape = inputs.shape
    return mixed.reshape(shape), igrad.reshape(shape), rgrad, lgrad, wgrad


def solution(mesh):
    placed = (
        P("dp", "seq", None),
        P("dp", "seq", None),
        P("seq", None),
        P("seq", None, None),
        P("seq", None, None),
    )
    return jax.shard_map(
        body,
        mesh=mesh,
        in_specs=placed,
        out_specs=(
            P("dp", "seq", None),
            P("dp", "seq", None),
            P("seq", None, None),
            P("seq", None, None),
            P("seq", None),
        ),
        check_vma=False,
    )
```

```python
import jax
import jax.numpy as jnp
from jax import lax
from jax.experimental import pallas as pl
from jax.experimental.pallas import tpu as pltpu
from jax.sharding import PartitionSpec as P

MESH = pl.DeviceIdType.MESH
F32 = jnp.float32
BF16 = jnp.bfloat16
N = 128
X4, Z4, Y4, C2 = 4, 4, 4, 2


def seq_of(x, z, y, c):
    return ((x * Z4 + z) * Y4 + y) * C2 + c


def dot(a, b, ca=1, cb=0):
    return lax.dot_general(a, b, (((ca,), (cb,)), ((), ())), preferred_element_type=F32)


def pack(x):
    return jnp.concatenate([x[:, :, :256], x[:, :, 256:]], axis=1).astype(BF16)


def unpack(w):
    w = w.astype(F32)
    return jnp.concatenate([w[:, :8, :], w[:, 8:, :]], axis=2)


def low_rows(shape):
    return lax.broadcasted_iota(jnp.int32, shape, 1) < 4


def interleave(t0, t1):
    low = low_rows(t0.shape)
    even = jnp.where(low, t0, pltpu.roll(t1, 4, 1))
    odd = jnp.where(low, pltpu.roll(t0, 4, 1), t1)
    return jnp.stack([even, odd], axis=1).reshape(2 * t0.shape[0], 8, t0.shape[2])


def deinterleave(w):
    pair = w.reshape(w.shape[0] // 2, 2, 8, w.shape[2])
    even, odd = pair[:, 0], pair[:, 1]
    low = low_rows(even.shape)
    return jnp.where(low, even, pltpu.roll(odd, 4, 1)), jnp.where(low, pltpu.roll(even, 4, 1), odd)


def loop(count, step):
    def run(i, carry):
        step(i)
        return carry

    lax.fori_loop(0, count, run, 0)


def at(i, size):
    return pl.ds(pl.multiple_of(i * size, size), size)


def mixer(
    x_hbm, u_hbm, w_ref, r_hbm, l_hbm,
    x_ref, u_ref, r4, back_ref, rg_own, rg_other, lg_own, lg_other, z_in,
    r_ref, l_ref, s1, r1, s2, r2, s3, r3, s4,
    wall, wm, m_ref, mt_ref, t_ref, g_ref, f_ref, v_ref, fg_ref, vg_ref,
    lg_big, lg_mid, core_in, plane_out, plane_in, z_out,
    send_sem, recv_sem, own_sem, w_sem, x_sem, in_sem,
):
    me = lax.axis_index("seq")
    dp = lax.axis_index("dp")
    x = lax.div(me, 32)
    z = lax.rem(lax.div(me, 8), 4)
    y = lax.rem(lax.div(me, 2), 4)
    c = lax.rem(me, 2)

    def remote(src, dst, send, recv, target, group=None):
        return pltpu.make_async_remote_copy(
            src_ref=src, dst_ref=dst, send_sem=send, recv_sem=recv,
            device_id=(dp if group is None else group, target), device_id_type=MESH,
        )

    def settle(ref, sem):
        pltpu.make_async_copy(ref, ref, sem).wait()

    def exchange(i, src, dst):
        pltpu.make_async_copy(src.at[me], dst.at[me], own_sem.at[i]).start()

        def send(k):
            d = lax.rem(me + k + 1, N)
            remote(src.at[d], dst.at[me], send_sem.at[i], recv_sem.at[i], d).start()

        loop(N - 1, send)

    def arrived(i, src, dst):
        pltpu.make_async_copy(src.at[me], dst.at[me], own_sem.at[i]).wait()
        settle(dst.at[pl.ds(0, N - 1)], recv_sem.at[i])

    def sent(i, src):
        settle(src.at[pl.ds(0, N - 1)], send_sem.at[i])

    def piece(j):
        return lax.rem(lax.div(me, 8) + j, 16)

    def load(j):
        b0 = pl.multiple_of(piece(j) * 32, 32)
        for a in range(2):
            for src, dst in ((x_hbm, x_ref), (u_hbm, u_ref)):
                pltpu.make_async_copy(
                    src.at[a, pl.ds(b0, 32)], dst.at[pl.ds(512 * a + b0, 32)], in_sem.at[j]
                ).start()

    loop(16, load)
    left_in = pltpu.make_async_copy(l_hbm, l_ref, in_sem.at[16])
    left_in.start()
    right_in = pltpu.make_async_copy(r_hbm, r_ref, in_sem.at[17])
    right_in.start()

    for m in range(2):
        rows = w_ref[:, 512 * m : 512 * m + 512].astype(F32).reshape(1, 8, 512)
        wall[x, z, y, c, :, 256 * m : 256 * m + 256] = pack(rows).reshape(16, 256)

    def spread(phase, block, targets):
        for t in targets:
            remote(block, block, w_sem.at[2 * phase], w_sem.at[2 * phase + 1], t).start()

    def spread_done(phase, like):
        settle(like, w_sem.at[2 * phase + 1])
        settle(like, w_sem.at[2 * phase])

    spread(0, wall.at[x, z, y, c], [seq_of(x, lax.rem(z + i, 4), y, c) for i in (1, 2, 3)])

    def second_grad(j):
        i = piece(j)
        settle(s1.at[pl.ds(0, 16)], in_sem.at[j])
        a0, a1 = at(i, 32), pl.ds(pl.multiple_of(512 + i * 32, 32), 32)
        for m in range(2):
            cols = slice(512 * m, 512 * m + 512)
            t0 = x_ref[a0, cols].astype(F32) * u_ref[a0, cols].astype(F32)
            t1 = x_ref[a1, cols].astype(F32) * u_ref[a1, cols].astype(F32)
            both = interleave(t0.reshape(4, 8, 512), t1.reshape(4, 8, 512))
            s1[at(i, 8), :, 256 * m : 256 * m + 256] = pack(both)

        def send(k):
            d = 8 * i + lax.rem(me + k, 8)

            @pl.when(d != me)
            def _():
                remote(s1.at[d], r1.at[me], send_sem.at[0], recv_sem.at[0], d).start()

        loop(8, send)

    loop(16, second_grad)
    pltpu.make_async_copy(s1.at[me], r1.at[me], own_sem.at[0]).start()

    def widen(b):
        select = (
            lax.broadcasted_iota(jnp.int32, (256, 1024), 1)
            == 4 * lax.broadcasted_iota(jnp.int32, (256, 1024), 0) + b
        ).astype(F32).astype(BF16)
        return select

    def place(i):
        row = lax.broadcasted_iota(jnp.int32, (256, 1024), 0) + i * 256
        col = lax.broadcasted_iota(jnp.int32, (256, 1024), 1)
        return (4 * lax.rem(col, 256) + lax.div(col, 256) == row).astype(F32).astype(BF16)

    def build(transposed, out):
        def wide(b):
            t_ref[at(b, 256), :] = dot(l_ref[b], widen(b), ca=0 if transposed else 1).astype(BF16)

        loop(4, wide)

        def rows(i):
            out[at(i, 256), :] = dot(place(i), t_ref[...]).astype(BF16)

        loop(4, rows)

    spread_done(0, wall.at[0, pl.ds(0, 3), 0, 0])
    spread(1, wall.at[x, :, y, c], [seq_of(lax.rem(x + i, 4), z, y, c) for i in (1, 2, 3)])
    left_in.wait()
    build(True, mt_ref)
    spread_done(1, wall.at[pl.ds(0, 3), :, 0, 0])
    spread(2, wall.at[:, :, y, c], [seq_of(x, z, lax.rem(y + i, 4), c) for i in (1, 2, 3)])
    build(False, m_ref)
    spread_done(2, wall.at[:, :, pl.ds(0, 3), 0])
    spread(3, wall.at[:, :, :, c], [seq_of(x, z, y, 1 - c)])
    spread_done(3, wall.at[:, :, :, 0])

    def unpack_weight(i):
        for m in range(2):
            part = wall[i, :, :, :, :, 256 * m : 256 * m + 256].reshape(32, 16, 256)
            wm[at(i, 256), 512 * m : 512 * m + 512] = unpack(part).reshape(256, 512).astype(BF16)

    loop(4, unpack_weight)

    def value(i):
        v_ref[at(i, 256), :] = dot(x_ref[at(i, 256), :], wm[...]).astype(BF16)

    loop(4, value)

    def first(i):
        for m in range(2):
            cols = slice(512 * m, 512 * m + 512)
            t0 = dot(r_ref[0, at(i, 256), :], v_ref[0:512, cols])
            t1 = dot(r_ref[1, at(i, 256), :], v_ref[512:1024, cols])
            both = interleave(t0.reshape(32, 8, 512), t1.reshape(32, 8, 512))
            s2[at(i, 64), :, 256 * m : 256 * m + 256] = pack(both)

    right_in.wait()
    loop(2, first)
    exchange(1, s2, r2)

    def unpack_all(src, dst):
        def step(i):
            for m in range(2):
                part = src[at(i, 16), :, 256 * m : 256 * m + 256]
                dst[at(i, 128), 512 * m : 512 * m + 512] = unpack(part).reshape(128, 512).astype(BF16)

        loop(8, step)

    def columns_product(big, cols_ref, out):
        def step(i):
            for m in range(2):
                t = dot(big[at(i, 256), :], cols_ref[:, 512 * m : 512 * m + 512])
                out[at(i, 32), :, 256 * m : 256 * m + 256] = pack(t.reshape(32, 8, 512))

        loop(4, step)

    arrived(0, s1, r1)
    unpack_all(r1, g_ref)
    columns_product(mt_ref, g_ref, s3)
    exchange(2, s3, r3)

    arrived(1, s2, r2)
    unpack_all(r2, f_ref)
    columns_product(m_ref, f_ref, s4)
    exchange(3, s4, r4)

    def left_all(i):
        rows = dot(g_ref[at(i, 256), :], f_ref[...], cb=1)
        row = lax.broadcasted_iota(jnp.int32, (256, 1024), 0)
        col = lax.broadcasted_iota(jnp.int32, (256, 1024), 1)
        lg_big[at(i, 256), :] = jnp.where(lax.rem(row, 4) == lax.rem(col, 4), rows, 0.0).astype(BF16)

    loop(4, left_all)

    def left_narrow(i):
        c_row = lax.broadcasted_iota(jnp.int32, (1024, 256), 0)
        c_col = lax.broadcasted_iota(jnp.int32, (1024, 256), 1)
        narrow = (lax.div(c_row, 4) == c_col).astype(F32).astype(BF16)
        lg_mid[at(i, 256), :] = dot(lg_big[at(i, 256), :], narrow).astype(BF16)

    loop(4, left_narrow)

    def left_place(b):
        row = lax.broadcasted_iota(jnp.int32, (256, 1024), 0)
        col = lax.broadcasted_iota(jnp.int32, (256, 1024), 1)
        take = (4 * row + b == col).astype(F32).astype(BF16)
        lg_own[b] = dot(take, lg_mid[...]).astype(BF16)

    loop(4, left_place)
    left_swap = remote(lg_own, lg_other, x_sem.at[0], x_sem.at[1], me, 1 - dp)
    left_swap.start()

    arrived(2, s3, r3)

    def first_grad(i):
        for m in range(2):
            t0, t1 = deinterleave(unpack(r3[at(i, 16), :, 256 * m : 256 * m + 256]))
            cols = slice(512 * m, 512 * m + 512)
            fg_ref[at(i, 64), cols] = t0.reshape(64, 512).astype(BF16)
            fg_ref[pl.ds(pl.multiple_of(512 + i * 64, 64), 64), cols] = t1.reshape(64, 512).astype(BF16)

    loop(8, first_grad)

    def right_part(i):
        rg_own[i] = dot(fg_ref[at(i, 512), :], v_ref[at(i, 512), :], cb=1).astype(BF16)

    loop(2, right_part)
    right_swap = remote(rg_own, rg_other, x_sem.at[2], x_sem.at[3], me, 1 - dp)
    right_swap.start()

    def value_grad(i):
        vg_ref[at(i, 512), :] = dot(r_ref[i], fg_ref[at(i, 512), :], ca=0).astype(BF16)

    loop(2, value_grad)

    def weight_part(i):
        for m in range(2):
            t = dot(x_ref[:, at(i, 256)], vg_ref[:, 512 * m : 512 * m + 512], ca=0)
            wall[i, :, :, :, :, 256 * m : 256 * m + 256] = pack(t.reshape(32, 8, 512)).reshape(4, 4, 2, 16, 256)

    loop(4, weight_part)
    to_core = remote(wall.at[:, :, :, 1 - c], core_in, x_sem.at[4], x_sem.at[5], seq_of(x, z, y, 1 - c))
    to_core.start()

    def back(i):
        back_ref[at(i, 256), :] = dot(vg_ref[at(i, 256), :], wm[...], cb=1)

    loop(2, back)
    to_core.wait()

    def add_core(i):
        mine = wall[i, :, :, c].astype(F32)
        plane_out[i] = (mine + core_in[i].astype(F32)).astype(BF16)

    loop(4, add_core)
    keep = pltpu.make_async_copy(plane_out.at[x, :, y], plane_in.at[x, y], own_sem.at[4])
    keep.start()
    for i in range(1, 16):
        tx, ty = lax.rem(x + i // 4, 4), lax.rem(y + i % 4, 4)
        remote(plane_out.at[tx, :, ty], plane_in.at[x, y], x_sem.at[6], x_sem.at[7], seq_of(tx, z, ty, c)).start()

    loop(2, lambda i: back(i + 2))
    keep.wait()
    settle(s1.at[pl.ds(0, 60)], x_sem.at[7])
    settle(s1.at[pl.ds(0, 60)], x_sem.at[6])

    def add_plane(i):
        total = jnp.zeros((16, 512), F32)
        for j in range(16):
            total = total + plane_in[j // 4, j % 4, i].astype(F32)
        z_out[i] = total.astype(BF16)

    loop(4, add_plane)
    zz = z * 2 + dp
    keep = pltpu.make_async_copy(z_out.at[z], z_in.at[zz], own_sem.at[5])
    keep.start()
    for i in range(1, 8):
        tz = lax.rem(zz + i, 8)
        th = lax.div(tz, 2)
        remote(z_out.at[th], z_in.at[zz], x_sem.at[8], x_sem.at[9], seq_of(x, th, y, c), lax.rem(tz, 2)).start()

    keep.wait()
    settle(s1.at[pl.ds(0, 7)], x_sem.at[9])
    settle(s1.at[pl.ds(0, 7)], x_sem.at[8])
    sent(0, s1)
    sent(1, s2)
    sent(2, s3)
    left_swap.wait()
    right_swap.wait()
    sent(3, s4)
    arrived(3, s4, r4)


def finish(
    x_ref, u_ref, r4, back_ref, rg_own, rg_other, lg_own, lg_other, z_in,
    mixed_hbm, igrad_hbm, rgrad_hbm, lgrad_hbm, wgrad_hbm,
    mixed, igrad, rgrad, lgrad, wgrad, sem,
):
    def moves(i):
        b = at(i, 64)
        return (
            pltpu.make_async_copy(mixed.at[:, b], mixed_hbm.at[:, b], sem.at[0, i]),
            pltpu.make_async_copy(igrad.at[:, b], igrad_hbm.at[:, b], sem.at[1, i]),
            pltpu.make_async_copy(rgrad.at[:, b], rgrad_hbm.at[:, b], sem.at[2, i]),
            pltpu.make_async_copy(lgrad.at[:, at(i, 32)], lgrad_hbm.at[:, at(i, 32)], sem.at[3, i]),
        )

    def part(i):
        b = at(i, 64)
        for a in range(2):
            rgrad[a, b, :] = rg_own[a, b, :].astype(F32) + rg_other[a, b, :].astype(F32)
        for m in range(2):
            cols = slice(512 * m, 512 * m + 512)
            parts = deinterleave(unpack(r4[at(i, 16), :, 256 * m : 256 * m + 256]))
            for a in range(2):
                rows = pl.ds(pl.multiple_of(512 * a + i * 64, 64), 64)
                second = parts[a].reshape(64, 512)
                mixed[a, b, cols] = (x_ref[rows, cols].astype(F32) * second).astype(BF16)
                igrad[a, b, cols] = (u_ref[rows, cols].astype(F32) * second + back_ref[rows, cols]).astype(BF16)
        q = at(i, 32)
        for k in range(4):
            lgrad[k, q, :] = lg_own[k, q, :].astype(F32) + lg_other[k, q, :].astype(F32)
        for move in moves(i):
            move.start()

    loop(8, part)
    total = jnp.zeros((16, 512), F32)
    for j in range(8):
        total = total + z_in[j].astype(F32)
    for m in range(2):
        for h in range(2):
            to = 512 * m + 256 * h
            wgrad[:, to : to + 256] = total[8 * h : 8 * h + 8, 256 * m : 256 * m + 256]
    last = pltpu.make_async_copy(wgrad, wgrad_hbm, sem.at[4, 0])
    last.start()

    def ended(i):
        for move in moves(i):
            move.wait()

    loop(8, ended)
    last.wait()


def body(inputs, cotangent, w_value, right_factor, left_factor):
    vmem = pl.BlockSpec(memory_space=pltpu.VMEM)
    hbm = pl.BlockSpec(memory_space=pl.ANY)

    def scratch(*shape, dtype=BF16):
        return pltpu.VMEM(shape, dtype)

    def array(*shape, dtype=BF16):
        return jax.ShapeDtypeStruct(shape, dtype)

    square = scratch(1024, 1024)
    wire = scratch(N, 16, 512)
    x2, u2 = inputs.reshape(2, 512, 1024), cotangent.reshape(2, 512, 1024)
    kept = pl.pallas_call(
        mixer,
        name="mixer",
        out_shape=(
            square,
            square,
            wire,
            scratch(1024, 1024, dtype=F32),
            scratch(2, 512, 512),
            scratch(2, 512, 512),
            scratch(4, 256, 256),
            scratch(4, 256, 256),
            scratch(8, 16, 512),
        ),
        in_specs=[hbm, hbm, vmem, hbm, hbm],
        out_specs=(vmem,) * 9,
        scratch_shapes=[scratch(2, 512, 512), scratch(4, 256, 256)]
        + [wire] * 7
        + [scratch(4, 4, 4, 2, 16, 512)]
        + [square] * 9
        + [square, scratch(1024, 256)]
        + [scratch(4, 4, 4, 16, 512)] * 3
        + [scratch(4, 16, 512)]
        + [pltpu.SemaphoreType.DMA((n,)) for n in (4, 4, 6, 8, 10, 18)],
        compiler_params=pltpu.CompilerParams(has_side_effects=True, vmem_limit_bytes=48 << 20),
        cost_estimate=pl.CostEstimate(flops=26_000_000_000, bytes_accessed=14_000_000, transcendentals=0),
    )(x2, u2, w_value, right_factor, left_factor)
    kept = [pltpu.with_memory_space_constraint(k, pltpu.VMEM) for k in kept]
    mixed, igrad, rgrad, lgrad, wgrad = pl.pallas_call(
        finish,
        name="finish",
        out_shape=(
            array(2, 512, 1024),
            array(2, 512, 1024),
            array(2, 512, 512, dtype=F32),
            array(4, 256, 256, dtype=F32),
            array(8, 1024, dtype=F32),
        ),
        in_specs=[vmem] * 9,
        out_specs=(hbm,) * 5,
        scratch_shapes=[
            scratch(2, 512, 1024),
            scratch(2, 512, 1024),
            scratch(2, 512, 512, dtype=F32),
            scratch(4, 256, 256, dtype=F32),
            scratch(8, 1024, dtype=F32),
            pltpu.SemaphoreType.DMA((5, 8)),
        ],
        compiler_params=pltpu.CompilerParams(vmem_limit_bytes=10 << 20),
        cost_estimate=pl.CostEstimate(flops=10_000_000, bytes_accessed=7_000_000, transcendentals=0),
    )(*kept)
    shape = inputs.shape
    return mixed.reshape(shape), igrad.reshape(shape), rgrad, lgrad, wgrad


def solution(mesh):
    placed = (
        P("dp", "seq", None),
        P("dp", "seq", None),
        P("seq", None),
        P("seq", None, None),
        P("seq", None, None),
    )
    return jax.shard_map(
        body,
        mesh=mesh,
        in_specs=placed,
        out_specs=(
            P("dp", "seq", None),
            P("dp", "seq", None),
            P("seq", None, None),
            P("seq", None, None),
            P("seq", None),
        ),
        check_vma=False,
    )
```

```python
import jax
import jax.numpy as jnp
from jax import lax
from jax.experimental import pallas as pl
from jax.experimental.pallas import tpu as pltpu
from jax.sharding import PartitionSpec as P

MESH = pl.DeviceIdType.MESH
F32 = jnp.float32
BF16 = jnp.bfloat16
N = 128
X4, Z4, Y4, C2 = 4, 4, 4, 2


def seq_of(x, z, y, c):
    return ((x * Z4 + z) * Y4 + y) * C2 + c


def dot(a, b, ca=1, cb=0):
    return lax.dot_general(a, b, (((ca,), (cb,)), ((), ())), preferred_element_type=F32)


def pack(x):
    return jnp.concatenate([x[:, :, :256], x[:, :, 256:]], axis=1).astype(BF16)


def unpack(w):
    w = w.astype(F32)
    return jnp.concatenate([w[:, :8, :], w[:, 8:, :]], axis=2)


def low_rows(shape):
    return lax.broadcasted_iota(jnp.int32, shape, 1) < 4


def interleave(t0, t1):
    low = low_rows(t0.shape)
    even = jnp.where(low, t0, pltpu.roll(t1, 4, 1))
    odd = jnp.where(low, pltpu.roll(t0, 4, 1), t1)
    return jnp.stack([even, odd], axis=1).reshape(2 * t0.shape[0], 8, t0.shape[2])


def deinterleave(w):
    pair = w.reshape(w.shape[0] // 2, 2, 8, w.shape[2])
    even, odd = pair[:, 0], pair[:, 1]
    low = low_rows(even.shape)
    return jnp.where(low, even, pltpu.roll(odd, 4, 1)), jnp.where(low, pltpu.roll(even, 4, 1), odd)


def loop(count, step):
    def run(i, carry):
        step(i)
        return carry

    lax.fori_loop(0, count, run, 0)


def at(i, size):
    return pl.ds(pl.multiple_of(i * size, size), size)


def mixer(
    x_hbm, u_hbm, w_ref, r_hbm, l_hbm,
    x_ref, u_ref, r4, back_ref, rg_own, rg_other, lg_own, lg_other, z_in,
    r_ref, l_ref, s1, r1, s2, r2, s3, r3, s4,
    wall, wm, m_ref, mt_ref, t_ref, g_ref, f_ref, v_ref, fg_ref, vg_ref,
    lg_big, lg_mid, core_in, plane_out, plane_in, z_out,
    send_sem, recv_sem, own_sem, w_sem, x_sem, in_sem,
):
    me = lax.axis_index("seq")
    dp = lax.axis_index("dp")
    x = lax.div(me, 32)
    z = lax.rem(lax.div(me, 8), 4)
    y = lax.rem(lax.div(me, 2), 4)
    c = lax.rem(me, 2)

    def remote(src, dst, send, recv, target, group=None):
        return pltpu.make_async_remote_copy(
            src_ref=src, dst_ref=dst, send_sem=send, recv_sem=recv,
            device_id=(dp if group is None else group, target), device_id_type=MESH,
        )

    def settle(ref, sem):
        pltpu.make_async_copy(ref, ref, sem).wait()

    def half(m):
        return pl.ds(256 * m, 256)

    def exchange(i, m, src, dst):
        pltpu.make_async_copy(src.at[me, :, half(m)], dst.at[me, :, half(m)], own_sem.at[2 * i + m]).start()

        def send(k):
            d = lax.rem(me + k + 1, N)
            remote(
                src.at[d, :, half(m)], dst.at[me, :, half(m)], send_sem.at[2 * i + m], recv_sem.at[2 * i + m], d
            ).start()

        loop(N - 1, send)

    def arrived(i, m, src, dst):
        pltpu.make_async_copy(src.at[me, :, half(m)], dst.at[me, :, half(m)], own_sem.at[2 * i + m]).wait()
        settle(dst.at[pl.ds(0, N - 1), :, half(m)], recv_sem.at[2 * i + m])

    def sent(i, src):
        for m in range(2):
            settle(src.at[pl.ds(0, N - 1), :, half(m)], send_sem.at[2 * i + m])

    def piece(j):
        return lax.rem(lax.div(me, 8) + j, 16)

    def load(j):
        b0 = pl.multiple_of(piece(j) * 32, 32)
        for a in range(2):
            for src, dst in ((x_hbm, x_ref), (u_hbm, u_ref)):
                pltpu.make_async_copy(
                    src.at[a, pl.ds(b0, 32)], dst.at[pl.ds(512 * a + b0, 32)], in_sem.at[j]
                ).start()

    loop(16, load)
    left_in = pltpu.make_async_copy(l_hbm, l_ref, in_sem.at[16])
    left_in.start()
    right_in = pltpu.make_async_copy(r_hbm, r_ref, in_sem.at[17])
    right_in.start()

    for m in range(2):
        rows = w_ref[:, 512 * m : 512 * m + 512].astype(F32).reshape(1, 8, 512)
        wall[x, z, y, c, :, 256 * m : 256 * m + 256] = pack(rows).reshape(16, 256)

    def spread(phase, block, targets):
        for t in targets:
            remote(block, block, w_sem.at[2 * phase], w_sem.at[2 * phase + 1], t).start()

    def spread_done(phase, like):
        settle(like, w_sem.at[2 * phase + 1])
        settle(like, w_sem.at[2 * phase])

    spread(0, wall.at[x, z, y, c], [seq_of(x, lax.rem(z + i, 4), y, c) for i in (1, 2, 3)])

    def second_grad(j):
        i = piece(j)
        settle(s1.at[pl.ds(0, 16)], in_sem.at[j])
        a0, a1 = at(i, 32), pl.ds(pl.multiple_of(512 + i * 32, 32), 32)
        for m in range(2):
            cols = slice(512 * m, 512 * m + 512)
            t0 = x_ref[a0, cols].astype(F32) * u_ref[a0, cols].astype(F32)
            t1 = x_ref[a1, cols].astype(F32) * u_ref[a1, cols].astype(F32)
            both = interleave(t0.reshape(4, 8, 512), t1.reshape(4, 8, 512))
            s1[at(i, 8), :, 256 * m : 256 * m + 256] = pack(both)

        def send(k):
            d = 8 * i + lax.rem(me + k, 8)

            @pl.when(d != me)
            def _():
                remote(s1.at[d, :, half(0)], r1.at[me, :, half(0)], send_sem.at[0], recv_sem.at[0], d).start()

        loop(8, send)

    loop(16, second_grad)
    pltpu.make_async_copy(s1.at[me, :, half(0)], r1.at[me, :, half(0)], own_sem.at[0]).start()
    exchange(0, 1, s1, r1)

    def widen(b):
        select = (
            lax.broadcasted_iota(jnp.int32, (256, 1024), 1)
            == 4 * lax.broadcasted_iota(jnp.int32, (256, 1024), 0) + b
        ).astype(F32).astype(BF16)
        return select

    def place(i):
        row = lax.broadcasted_iota(jnp.int32, (256, 1024), 0) + i * 256
        col = lax.broadcasted_iota(jnp.int32, (256, 1024), 1)
        return (4 * lax.rem(col, 256) + lax.div(col, 256) == row).astype(F32).astype(BF16)

    def build(transposed, out):
        def wide(b):
            t_ref[at(b, 256), :] = dot(l_ref[b], widen(b), ca=0 if transposed else 1).astype(BF16)

        loop(4, wide)

        def rows(i):
            out[at(i, 256), :] = dot(place(i), t_ref[...]).astype(BF16)

        loop(4, rows)

    def unpack_cols(src, dst, m):
        def step(i):
            part = unpack(src[at(i, 16), :, 256 * m : 256 * m + 256])
            dst[at(i, 128), 512 * m : 512 * m + 512] = part.reshape(128, 512).astype(BF16)

        loop(8, step)

    def columns_product(big, cols_ref, out, m):
        def step(i):
            t = dot(big[at(i, 256), :], cols_ref[:, 512 * m : 512 * m + 512])
            out[at(i, 32), :, 256 * m : 256 * m + 256] = pack(t.reshape(32, 8, 512))

        loop(4, step)

    def first_grad_columns(m):
        arrived(0, m, s1, r1)
        unpack_cols(r1, g_ref, m)
        columns_product(mt_ref, g_ref, s3, m)
        exchange(2, m, s3, r3)

    def second_columns(m):
        arrived(1, m, s2, r2)
        unpack_cols(r2, f_ref, m)
        columns_product(m_ref, f_ref, s4, m)
        exchange(3, m, s4, r4)

    def first_grad(m):
        arrived(2, m, s3, r3)

        def step(i):
            t0, t1 = deinterleave(unpack(r3[at(i, 16), :, 256 * m : 256 * m + 256]))
            cols = slice(512 * m, 512 * m + 512)
            fg_ref[at(i, 64), cols] = t0.reshape(64, 512).astype(BF16)
            fg_ref[pl.ds(pl.multiple_of(512 + i * 64, 64), 64), cols] = t1.reshape(64, 512).astype(BF16)

        loop(8, step)

    spread_done(0, wall.at[0, pl.ds(0, 3), 0, 0])
    spread(1, wall.at[x, :, y, c], [seq_of(lax.rem(x + i, 4), z, y, c) for i in (1, 2, 3)])
    left_in.wait()
    build(True, mt_ref)
    spread_done(1, wall.at[pl.ds(0, 3), :, 0, 0])
    spread(2, wall.at[:, :, y, c], [seq_of(x, z, lax.rem(y + i, 4), c) for i in (1, 2, 3)])
    first_grad_columns(0)
    spread_done(2, wall.at[:, :, pl.ds(0, 3), 0])
    spread(3, wall.at[:, :, :, c], [seq_of(x, z, y, 1 - c)])
    right_in.wait()
    spread_done(3, wall.at[:, :, :, 0])

    def unpack_weight(i):
        for m in range(2):
            part = wall[i, :, :, :, :, 256 * m : 256 * m + 256].reshape(32, 16, 256)
            wm[at(i, 256), 512 * m : 512 * m + 512] = unpack(part).reshape(256, 512).astype(BF16)

    loop(4, unpack_weight)

    def value(i):
        v_ref[at(i, 256), :] = dot(x_ref[at(i, 256), :], wm[...]).astype(BF16)

    loop(4, value)

    def first(m):
        def step(i):
            cols = slice(512 * m, 512 * m + 512)
            t0 = dot(r_ref[0, at(i, 256), :], v_ref[0:512, cols])
            t1 = dot(r_ref[1, at(i, 256), :], v_ref[512:1024, cols])
            both = interleave(t0.reshape(32, 8, 512), t1.reshape(32, 8, 512))
            s2[at(i, 64), :, 256 * m : 256 * m + 256] = pack(both)

        loop(2, step)
        exchange(1, m, s2, r2)

    first(0)
    first(1)
    first_grad_columns(1)
    build(False, m_ref)
    first_grad(0)
    second_columns(0)
    second_columns(1)

    def left_all(i):
        rows = dot(g_ref[at(i, 256), :], f_ref[...], cb=1)
        row = lax.broadcasted_iota(jnp.int32, (256, 1024), 0)
        col = lax.broadcasted_iota(jnp.int32, (256, 1024), 1)
        lg_big[at(i, 256), :] = jnp.where(lax.rem(row, 4) == lax.rem(col, 4), rows, 0.0).astype(BF16)

    loop(4, left_all)

    def left_narrow(i):
        c_row = lax.broadcasted_iota(jnp.int32, (1024, 256), 0)
        c_col = lax.broadcasted_iota(jnp.int32, (1024, 256), 1)
        narrow = (lax.div(c_row, 4) == c_col).astype(F32).astype(BF16)
        lg_mid[at(i, 256), :] = dot(lg_big[at(i, 256), :], narrow).astype(BF16)

    loop(4, left_narrow)

    def left_place(b):
        row = lax.broadcasted_iota(jnp.int32, (256, 1024), 0)
        col = lax.broadcasted_iota(jnp.int32, (256, 1024), 1)
        take = (4 * row + b == col).astype(F32).astype(BF16)
        lg_own[b] = dot(take, lg_mid[...]).astype(BF16)

    loop(4, left_place)
    left_swap = remote(lg_own, lg_other, x_sem.at[0], x_sem.at[1], me, 1 - dp)
    left_swap.start()

    first_grad(1)

    def right_part(i):
        rg_own[i] = dot(fg_ref[at(i, 512), :], v_ref[at(i, 512), :], cb=1).astype(BF16)

    loop(2, right_part)
    right_swap = remote(rg_own, rg_other, x_sem.at[2], x_sem.at[3], me, 1 - dp)
    right_swap.start()

    def value_grad(i):
        vg_ref[at(i, 512), :] = dot(r_ref[i], fg_ref[at(i, 512), :], ca=0).astype(BF16)

    loop(2, value_grad)

    def weight_part(i):
        for m in range(2):
            t = dot(x_ref[:, at(i, 256)], vg_ref[:, 512 * m : 512 * m + 512], ca=0)
            wall[i, :, :, :, :, 256 * m : 256 * m + 256] = pack(t.reshape(32, 8, 512)).reshape(4, 4, 2, 16, 256)

    loop(4, weight_part)
    to_core = remote(wall.at[:, :, :, 1 - c], core_in, x_sem.at[4], x_sem.at[5], seq_of(x, z, y, 1 - c))
    to_core.start()

    def back(i):
        back_ref[at(i, 256), :] = dot(vg_ref[at(i, 256), :], wm[...], cb=1)

    loop(2, back)
    to_core.wait()

    def add_core(i):
        mine = wall[i, :, :, c].astype(F32)
        plane_out[i] = (mine + core_in[i].astype(F32)).astype(BF16)

    loop(4, add_core)
    keep = pltpu.make_async_copy(plane_out.at[x, :, y], plane_in.at[x, y], own_sem.at[8])
    keep.start()
    for i in range(1, 16):
        tx, ty = lax.rem(x + i // 4, 4), lax.rem(y + i % 4, 4)
        remote(plane_out.at[tx, :, ty], plane_in.at[x, y], x_sem.at[6], x_sem.at[7], seq_of(tx, z, ty, c)).start()

    loop(2, lambda i: back(i + 2))
    keep.wait()
    settle(s1.at[pl.ds(0, 60)], x_sem.at[7])
    settle(s1.at[pl.ds(0, 60)], x_sem.at[6])

    def add_plane(i):
        total = jnp.zeros((16, 512), F32)
        for j in range(16):
            total = total + plane_in[j // 4, j % 4, i].astype(F32)
        z_out[i] = total.astype(BF16)

    loop(4, add_plane)
    zz = z * 2 + dp
    keep = pltpu.make_async_copy(z_out.at[z], z_in.at[zz], own_sem.at[9])
    keep.start()
    for i in range(1, 8):
        tz = lax.rem(zz + i, 8)
        th = lax.div(tz, 2)
        remote(z_out.at[th], z_in.at[zz], x_sem.at[8], x_sem.at[9], seq_of(x, th, y, c), lax.rem(tz, 2)).start()

    keep.wait()
    settle(s1.at[pl.ds(0, 7)], x_sem.at[9])
    settle(s1.at[pl.ds(0, 7)], x_sem.at[8])
    sent(0, s1)
    sent(1, s2)
    sent(2, s3)
    left_swap.wait()
    right_swap.wait()
    sent(3, s4)
    arrived(3, 0, s4, r4)
    arrived(3, 1, s4, r4)


def finish(
    x_ref, u_ref, r4, back_ref, rg_own, rg_other, lg_own, lg_other, z_in,
    mixed_hbm, igrad_hbm, rgrad_hbm, lgrad_hbm, wgrad_hbm,
    mixed, igrad, rgrad, lgrad, wgrad, sem,
):
    def moves(i):
        b = at(i, 64)
        return (
            pltpu.make_async_copy(mixed.at[:, b], mixed_hbm.at[:, b], sem.at[0, i]),
            pltpu.make_async_copy(igrad.at[:, b], igrad_hbm.at[:, b], sem.at[1, i]),
            pltpu.make_async_copy(rgrad.at[:, b], rgrad_hbm.at[:, b], sem.at[2, i]),
            pltpu.make_async_copy(lgrad.at[:, at(i, 32)], lgrad_hbm.at[:, at(i, 32)], sem.at[3, i]),
        )

    def part(i):
        b = at(i, 64)
        for a in range(2):
            rgrad[a, b, :] = rg_own[a, b, :].astype(F32) + rg_other[a, b, :].astype(F32)
        for m in range(2):
            cols = slice(512 * m, 512 * m + 512)
            parts = deinterleave(unpack(r4[at(i, 16), :, 256 * m : 256 * m + 256]))
            for a in range(2):
                rows = pl.ds(pl.multiple_of(512 * a + i * 64, 64), 64)
                second = parts[a].reshape(64, 512)
                mixed[a, b, cols] = (x_ref[rows, cols].astype(F32) * second).astype(BF16)
                igrad[a, b, cols] = (u_ref[rows, cols].astype(F32) * second + back_ref[rows, cols]).astype(BF16)
        q = at(i, 32)
        for k in range(4):
            lgrad[k, q, :] = lg_own[k, q, :].astype(F32) + lg_other[k, q, :].astype(F32)
        for move in moves(i):
            move.start()

    loop(8, part)
    total = jnp.zeros((16, 512), F32)
    for j in range(8):
        total = total + z_in[j].astype(F32)
    for m in range(2):
        for h in range(2):
            to = 512 * m + 256 * h
            wgrad[:, to : to + 256] = total[8 * h : 8 * h + 8, 256 * m : 256 * m + 256]
    last = pltpu.make_async_copy(wgrad, wgrad_hbm, sem.at[4, 0])
    last.start()

    def ended(i):
        for move in moves(i):
            move.wait()

    loop(8, ended)
    last.wait()


def body(inputs, cotangent, w_value, right_factor, left_factor):
    vmem = pl.BlockSpec(memory_space=pltpu.VMEM)
    hbm = pl.BlockSpec(memory_space=pl.ANY)

    def scratch(*shape, dtype=BF16):
        return pltpu.VMEM(shape, dtype)

    def array(*shape, dtype=BF16):
        return jax.ShapeDtypeStruct(shape, dtype)

    square = scratch(1024, 1024)
    wire = scratch(N, 16, 512)
    x2, u2 = inputs.reshape(2, 512, 1024), cotangent.reshape(2, 512, 1024)
    kept = pl.pallas_call(
        mixer,
        name="mixer",
        out_shape=(
            square,
            square,
            wire,
            scratch(1024, 1024, dtype=F32),
            scratch(2, 512, 512),
            scratch(2, 512, 512),
            scratch(4, 256, 256),
            scratch(4, 256, 256),
            scratch(8, 16, 512),
        ),
        in_specs=[hbm, hbm, vmem, hbm, hbm],
        out_specs=(vmem,) * 9,
        scratch_shapes=[scratch(2, 512, 512), scratch(4, 256, 256)]
        + [wire] * 7
        + [scratch(4, 4, 4, 2, 16, 512)]
        + [square] * 9
        + [square, scratch(1024, 256)]
        + [scratch(4, 4, 4, 16, 512)] * 3
        + [scratch(4, 16, 512)]
        + [pltpu.SemaphoreType.DMA((n,)) for n in (8, 8, 10, 8, 10, 18)],
        compiler_params=pltpu.CompilerParams(has_side_effects=True, vmem_limit_bytes=48 << 20),
        cost_estimate=pl.CostEstimate(flops=26_000_000_000, bytes_accessed=14_000_000, transcendentals=0),
    )(x2, u2, w_value, right_factor, left_factor)
    kept = [pltpu.with_memory_space_constraint(k, pltpu.VMEM) for k in kept]
    mixed, igrad, rgrad, lgrad, wgrad = pl.pallas_call(
        finish,
        name="finish",
        out_shape=(
            array(2, 512, 1024),
            array(2, 512, 1024),
            array(2, 512, 512, dtype=F32),
            array(4, 256, 256, dtype=F32),
            array(8, 1024, dtype=F32),
        ),
        in_specs=[vmem] * 9,
        out_specs=(hbm,) * 5,
        scratch_shapes=[
            scratch(2, 512, 1024),
            scratch(2, 512, 1024),
            scratch(2, 512, 512, dtype=F32),
            scratch(4, 256, 256, dtype=F32),
            scratch(8, 1024, dtype=F32),
            pltpu.SemaphoreType.DMA((5, 8)),
        ],
        compiler_params=pltpu.CompilerParams(vmem_limit_bytes=10 << 20),
        cost_estimate=pl.CostEstimate(flops=10_000_000, bytes_accessed=7_000_000, transcendentals=0),
    )(*kept)
    shape = inputs.shape
    return mixed.reshape(shape), igrad.reshape(shape), rgrad, lgrad, wgrad


def solution(mesh):
    placed = (
        P("dp", "seq", None),
        P("dp", "seq", None),
        P("seq", None),
        P("seq", None, None),
        P("seq", None, None),
    )
    return jax.shard_map(
        body,
        mesh=mesh,
        in_specs=placed,
        out_specs=(
            P("dp", "seq", None),
            P("dp", "seq", None),
            P("seq", None, None),
            P("seq", None, None),
            P("seq", None),
        ),
        check_vma=False,
    )
```

```python
import jax
import jax.numpy as jnp
from jax import lax
from jax.experimental import pallas as pl
from jax.experimental.pallas import tpu as pltpu
from jax.sharding import PartitionSpec as P

MESH = pl.DeviceIdType.MESH
F32 = jnp.float32
BF16 = jnp.bfloat16
N = 128
X4, Z4, Y4, C2 = 4, 4, 4, 2


def seq_of(x, z, y, c):
    return ((x * Z4 + z) * Y4 + y) * C2 + c


def dot(a, b, ca=1, cb=0):
    return lax.dot_general(a, b, (((ca,), (cb,)), ((), ())), preferred_element_type=F32)


def pack(x):
    return jnp.concatenate([x[:, :, :256], x[:, :, 256:]], axis=1).astype(BF16)


def unpack(w):
    w = w.astype(F32)
    return jnp.concatenate([w[:, :8, :], w[:, 8:, :]], axis=2)


def low_rows(shape):
    return lax.broadcasted_iota(jnp.int32, shape, 1) < 4


def interleave(t0, t1):
    low = low_rows(t0.shape)
    even = jnp.where(low, t0, pltpu.roll(t1, 4, 1))
    odd = jnp.where(low, pltpu.roll(t0, 4, 1), t1)
    return jnp.stack([even, odd], axis=1).reshape(2 * t0.shape[0], 8, t0.shape[2])


def deinterleave(w):
    pair = w.reshape(w.shape[0] // 2, 2, 8, w.shape[2])
    even, odd = pair[:, 0], pair[:, 1]
    low = low_rows(even.shape)
    return jnp.where(low, even, pltpu.roll(odd, 4, 1)), jnp.where(low, pltpu.roll(even, 4, 1), odd)


def loop(count, step):
    def run(i, carry):
        step(i)
        return carry

    lax.fori_loop(0, count, run, 0)


def at(i, size):
    return pl.ds(pl.multiple_of(i * size, size), size)


def results(i, m, x_ref, u_ref, r4, back_ref, mixed, igrad):
    parts = deinterleave(unpack(r4[at(i, 16), :, 256 * m : 256 * m + 256]))
    cols = slice(512 * m, 512 * m + 512)
    for a in range(2):
        rows = pl.ds(pl.multiple_of(512 * a + i * 64, 64), 64)
        second = parts[a].reshape(64, 512)
        mixed[a, at(i, 64), :] = (x_ref[rows, cols].astype(F32) * second).astype(BF16)
        igrad[a, at(i, 64), :] = (u_ref[rows, cols].astype(F32) * second + back_ref[rows, cols]).astype(BF16)


def mixer(
    x_hbm, u_hbm, w_ref, r_hbm, l_hbm,
    x_ref, u_ref, r4, back_ref, rg_own, rg_other, lg_own, lg_other, z_in, mixed_0, igrad_0,
    r_ref, l_ref, s1, r1, s2, r2, s3, r3, s4,
    wall, wm, m_ref, mt_ref, t_ref, g_ref, f_ref, v_ref, fg_ref, vg_ref,
    lg_mid, core_in, plane_out, plane_in, z_out,
    send_sem, recv_sem, own_sem, w_sem, x_sem, in_sem,
):
    me = lax.axis_index("seq")
    dp = lax.axis_index("dp")
    x = lax.div(me, 32)
    z = lax.rem(lax.div(me, 8), 4)
    y = lax.rem(lax.div(me, 2), 4)
    c = lax.rem(me, 2)

    def remote(src, dst, send, recv, target, group=None):
        return pltpu.make_async_remote_copy(
            src_ref=src, dst_ref=dst, send_sem=send, recv_sem=recv,
            device_id=(dp if group is None else group, target), device_id_type=MESH,
        )

    def settle(ref, sem):
        pltpu.make_async_copy(ref, ref, sem).wait()

    def half(m):
        return pl.ds(256 * m, 256)

    def exchange(i, m, src, dst):
        pltpu.make_async_copy(src.at[me, :, half(m)], dst.at[me, :, half(m)], own_sem.at[2 * i + m]).start()

        def send(k):
            d = lax.rem(me + k + 1, N)
            remote(
                src.at[d, :, half(m)], dst.at[me, :, half(m)], send_sem.at[2 * i + m], recv_sem.at[2 * i + m], d
            ).start()

        loop(N - 1, send)

    def arrived(i, m, src, dst):
        pltpu.make_async_copy(src.at[me, :, half(m)], dst.at[me, :, half(m)], own_sem.at[2 * i + m]).wait()
        settle(dst.at[pl.ds(0, N - 1), :, half(m)], recv_sem.at[2 * i + m])

    def sent(i, src):
        for m in range(2):
            settle(src.at[pl.ds(0, N - 1), :, half(m)], send_sem.at[2 * i + m])

    def piece(j):
        return lax.rem(lax.div(me, 8) + j, 16)

    def load(j):
        b0 = pl.multiple_of(piece(j) * 32, 32)
        for a in range(2):
            for src, dst in ((x_hbm, x_ref), (u_hbm, u_ref)):
                pltpu.make_async_copy(
                    src.at[a, pl.ds(b0, 32)], dst.at[pl.ds(512 * a + b0, 32)], in_sem.at[j]
                ).start()

    loop(16, load)
    left_in = pltpu.make_async_copy(l_hbm, l_ref, in_sem.at[16])
    left_in.start()
    right_in = pltpu.make_async_copy(r_hbm, r_ref, in_sem.at[17])
    right_in.start()

    ready = pltpu.get_barrier_semaphore()

    def greet(group, target):
        pl.semaphore_signal(ready, inc=1, device_id=(group, target), device_id_type=MESH)

    loop(N - 1, lambda k: greet(dp, lax.rem(me + k + 1, N)))
    for i in range(4):
        greet(1 - dp, seq_of(x, lax.rem(z + i, 4), y, c))

    def second_grad(j):
        i = piece(j)
        settle(s1.at[pl.ds(0, 16)], in_sem.at[j])
        a0, a1 = at(i, 32), pl.ds(pl.multiple_of(512 + i * 32, 32), 32)
        for m in range(2):
            cols = slice(512 * m, 512 * m + 512)
            t0 = x_ref[a0, cols].astype(F32) * u_ref[a0, cols].astype(F32)
            t1 = x_ref[a1, cols].astype(F32) * u_ref[a1, cols].astype(F32)
            both = interleave(t0.reshape(4, 8, 512), t1.reshape(4, 8, 512))
            s1[at(i, 8), :, 256 * m : 256 * m + 256] = pack(both)

    def second_grad_out(j):
        def send(k):
            d = 8 * piece(j) + lax.rem(me + k, 8)

            @pl.when(d != me)
            def _():
                remote(s1.at[d, :, half(0)], r1.at[me, :, half(0)], send_sem.at[0], recv_sem.at[0], d).start()

        loop(8, send)

    for m in range(2):
        rows = w_ref[:, 512 * m : 512 * m + 512].astype(F32).reshape(1, 8, 512)
        wall[x, z, y, c, :, 256 * m : 256 * m + 256] = pack(rows).reshape(16, 256)

    def spread(phase, block, targets):
        for t in targets:
            remote(block, block, w_sem.at[2 * phase], w_sem.at[2 * phase + 1], t).start()

    def spread_done(phase, like):
        settle(like, w_sem.at[2 * phase + 1])
        settle(like, w_sem.at[2 * phase])


    loop(4, lambda j: second_grad(j))
    pl.semaphore_wait(ready, N + 3)
    spread(0, wall.at[x, z, y, c], [seq_of(x, lax.rem(z + i, 4), y, c) for i in (1, 2, 3)])

    def ahead(j):
        second_grad_out(j)
        second_grad(j + 4)

    loop(12, ahead)
    loop(4, lambda j: second_grad_out(j + 12))
    pltpu.make_async_copy(s1.at[me, :, half(0)], r1.at[me, :, half(0)], own_sem.at[0]).start()
    exchange(0, 1, s1, r1)

    def widen(b):
        select = (
            lax.broadcasted_iota(jnp.int32, (256, 1024), 1)
            == 4 * lax.broadcasted_iota(jnp.int32, (256, 1024), 0) + b
        ).astype(F32).astype(BF16)
        return select

    def place(i):
        row = lax.broadcasted_iota(jnp.int32, (256, 1024), 0) + i * 256
        col = lax.broadcasted_iota(jnp.int32, (256, 1024), 1)
        return (4 * lax.rem(col, 256) + lax.div(col, 256) == row).astype(F32).astype(BF16)

    def build(transposed, out):
        def wide(b):
            t_ref[at(b, 256), :] = dot(l_ref[b], widen(b), ca=0 if transposed else 1).astype(BF16)

        loop(4, wide)

        def rows(i):
            out[at(i, 256), :] = dot(place(i), t_ref[...]).astype(BF16)

        loop(4, rows)

    def unpack_cols(src, dst, m):
        def step(i):
            part = unpack(src[at(i, 16), :, 256 * m : 256 * m + 256])
            dst[at(i, 128), 512 * m : 512 * m + 512] = part.reshape(128, 512).astype(BF16)

        loop(8, step)

    def columns_product(big, cols_ref, out, m):
        def step(i):
            t = dot(big[at(i, 256), :], cols_ref[:, 512 * m : 512 * m + 512])
            out[at(i, 32), :, 256 * m : 256 * m + 256] = pack(t.reshape(32, 8, 512))

        loop(4, step)

    def first_grad_columns(m):
        arrived(0, m, s1, r1)
        unpack_cols(r1, g_ref, m)
        columns_product(mt_ref, g_ref, s3, m)
        exchange(2, m, s3, r3)

    def second_columns(m):
        arrived(1, m, s2, r2)
        unpack_cols(r2, f_ref, m)
        columns_product(m_ref, f_ref, s4, m)
        exchange(3, m, s4, r4)

    def first_grad(m):
        arrived(2, m, s3, r3)

        def step(i):
            t0, t1 = deinterleave(unpack(r3[at(i, 16), :, 256 * m : 256 * m + 256]))
            cols = slice(512 * m, 512 * m + 512)
            fg_ref[at(i, 64), cols] = t0.reshape(64, 512).astype(BF16)
            fg_ref[pl.ds(pl.multiple_of(512 + i * 64, 64), 64), cols] = t1.reshape(64, 512).astype(BF16)

        loop(8, step)

    spread_done(0, wall.at[0, pl.ds(0, 3), 0, 0])
    spread(1, wall.at[x, :, y, c], [seq_of(lax.rem(x + i, 4), z, y, c) for i in (1, 2, 3)])
    left_in.wait()
    build(True, mt_ref)
    spread_done(1, wall.at[pl.ds(0, 3), :, 0, 0])
    spread(2, wall.at[:, :, y, c], [seq_of(x, z, lax.rem(y + i, 4), c) for i in (1, 2, 3)])
    first_grad_columns(0)
    spread_done(2, wall.at[:, :, pl.ds(0, 3), 0])
    spread(3, wall.at[:, :, :, c], [seq_of(x, z, y, 1 - c)])
    right_in.wait()
    spread_done(3, wall.at[:, :, :, 0])

    def unpack_weight(i):
        for m in range(2):
            part = wall[i, :, :, :, :, 256 * m : 256 * m + 256].reshape(32, 16, 256)
            wm[at(i, 256), 512 * m : 512 * m + 512] = unpack(part).reshape(256, 512).astype(BF16)

    loop(4, unpack_weight)

    def value(i):
        v_ref[at(i, 256), :] = dot(x_ref[at(i, 256), :], wm[...]).astype(BF16)

    loop(4, value)

    def first(m):
        def step(i):
            cols = slice(512 * m, 512 * m + 512)
            t0 = dot(r_ref[0, at(i, 256), :], v_ref[0:512, cols])
            t1 = dot(r_ref[1, at(i, 256), :], v_ref[512:1024, cols])
            both = interleave(t0.reshape(32, 8, 512), t1.reshape(32, 8, 512))
            s2[at(i, 64), :, 256 * m : 256 * m + 256] = pack(both)

        loop(2, step)
        exchange(1, m, s2, r2)

    first(0)
    first(1)
    first_grad_columns(1)
    build(False, m_ref)
    first_grad(0)
    second_columns(0)
    second_columns(1)

    def left_all(i):
        rows = dot(g_ref[at(i, 256), :], f_ref[...], cb=1)
        row = lax.broadcasted_iota(jnp.int32, (256, 1024), 0)
        col = lax.broadcasted_iota(jnp.int32, (256, 1024), 1)
        t_ref[at(i, 256), :] = jnp.where(lax.rem(row, 4) == lax.rem(col, 4), rows, 0.0).astype(BF16)

    loop(4, left_all)

    def left_narrow(i):
        c_row = lax.broadcasted_iota(jnp.int32, (1024, 256), 0)
        c_col = lax.broadcasted_iota(jnp.int32, (1024, 256), 1)
        narrow = (lax.div(c_row, 4) == c_col).astype(F32).astype(BF16)
        lg_mid[at(i, 256), :] = dot(t_ref[at(i, 256), :], narrow).astype(BF16)

    loop(4, left_narrow)

    def left_place(b):
        row = lax.broadcasted_iota(jnp.int32, (256, 1024), 0)
        col = lax.broadcasted_iota(jnp.int32, (256, 1024), 1)
        take = (4 * row + b == col).astype(F32).astype(BF16)
        lg_own[b] = dot(take, lg_mid[...]).astype(BF16)

    loop(4, left_place)
    left_swap = remote(lg_own, lg_other, x_sem.at[0], x_sem.at[1], me, 1 - dp)
    left_swap.start()

    first_grad(1)

    def right_part(i):
        rg_own[i] = dot(fg_ref[at(i, 512), :], v_ref[at(i, 512), :], cb=1).astype(BF16)

    loop(2, right_part)
    right_swap = remote(rg_own, rg_other, x_sem.at[2], x_sem.at[3], me, 1 - dp)
    right_swap.start()

    def value_grad(i):
        vg_ref[at(i, 512), :] = dot(r_ref[i], fg_ref[at(i, 512), :], ca=0).astype(BF16)

    loop(2, value_grad)

    def weight_part(i):
        for m in range(2):
            t = dot(x_ref[:, at(i, 256)], vg_ref[:, 512 * m : 512 * m + 512], ca=0)
            wall[i, :, :, :, :, 256 * m : 256 * m + 256] = pack(t.reshape(32, 8, 512)).reshape(4, 4, 2, 16, 256)

    loop(4, weight_part)
    to_core = remote(wall.at[:, :, :, 1 - c], core_in, x_sem.at[4], x_sem.at[5], seq_of(x, z, y, 1 - c))
    to_core.start()

    def back(i):
        back_ref[at(i, 256), :] = dot(vg_ref[at(i, 256), :], wm[...], cb=1)

    loop(2, back)
    to_core.wait()

    def add_core(i):
        mine = wall[i, :, :, c].astype(F32)
        plane_out[i] = (mine + core_in[i].astype(F32)).astype(BF16)

    loop(4, add_core)
    keep = pltpu.make_async_copy(plane_out.at[x, :, y], plane_in.at[x, y], own_sem.at[8])
    keep.start()
    for i in range(1, 16):
        tx, ty = lax.rem(x + i // 4, 4), lax.rem(y + i % 4, 4)
        remote(plane_out.at[tx, :, ty], plane_in.at[x, y], x_sem.at[6], x_sem.at[7], seq_of(tx, z, ty, c)).start()

    loop(2, lambda i: back(i + 2))
    keep.wait()
    settle(s1.at[pl.ds(0, 60)], x_sem.at[7])
    settle(s1.at[pl.ds(0, 60)], x_sem.at[6])

    def add_plane(i):
        total = jnp.zeros((16, 512), F32)
        for j in range(16):
            total = total + plane_in[j // 4, j % 4, i].astype(F32)
        z_out[i] = total.astype(BF16)

    loop(4, add_plane)
    zz = z * 2 + dp
    keep = pltpu.make_async_copy(z_out.at[z], z_in.at[zz], own_sem.at[9])
    keep.start()
    for i in range(1, 8):
        tz = lax.rem(zz + i, 8)
        th = lax.div(tz, 2)
        remote(z_out.at[th], z_in.at[zz], x_sem.at[8], x_sem.at[9], seq_of(x, th, y, c), lax.rem(tz, 2)).start()

    arrived(3, 0, s4, r4)

    def results_0(i):
        results(i, 0, x_ref, u_ref, r4, back_ref, mixed_0, igrad_0)

    loop(8, results_0)

    keep.wait()
    settle(s1.at[pl.ds(0, 7)], x_sem.at[9])
    settle(s1.at[pl.ds(0, 7)], x_sem.at[8])
    sent(0, s1)
    sent(1, s2)
    sent(2, s3)
    left_swap.wait()
    right_swap.wait()
    sent(3, s4)
    arrived(3, 1, s4, r4)


def finish(
    x_ref, u_ref, r4, back_ref, rg_own, rg_other, lg_own, lg_other, z_in, mixed_0, igrad_0,
    mixed_hbm, igrad_hbm, rgrad_hbm, lgrad_hbm, wgrad_hbm,
    mixed_1, igrad_1, rgrad, lgrad, wgrad, sem,
):
    def moves(i):
        b, q = at(i, 64), at(i, 32)
        return (
            pltpu.make_async_copy(mixed_1.at[:, b], mixed_hbm.at[:, b, pl.ds(512, 512)], sem.at[0, i]),
            pltpu.make_async_copy(igrad_1.at[:, b], igrad_hbm.at[:, b, pl.ds(512, 512)], sem.at[1, i]),
            pltpu.make_async_copy(rgrad.at[:, b], rgrad_hbm.at[:, b], sem.at[2, i]),
            pltpu.make_async_copy(lgrad.at[:, q], lgrad_hbm.at[:, q], sem.at[3, i]),
        )

    early = (
        pltpu.make_async_copy(mixed_0, mixed_hbm.at[:, :, pl.ds(0, 512)], sem.at[4, 1]),
        pltpu.make_async_copy(igrad_0, igrad_hbm.at[:, :, pl.ds(0, 512)], sem.at[4, 2]),
    )
    for move in early:
        move.start()

    def part(i):
        b, q = at(i, 64), at(i, 32)
        for a in range(2):
            rgrad[a, b, :] = rg_own[a, b, :].astype(F32) + rg_other[a, b, :].astype(F32)
        for k in range(4):
            lgrad[k, q, :] = lg_own[k, q, :].astype(F32) + lg_other[k, q, :].astype(F32)
        results(i, 1, x_ref, u_ref, r4, back_ref, mixed_1, igrad_1)
        for move in moves(i):
            move.start()

    loop(8, part)
    total = jnp.zeros((16, 512), F32)
    for j in range(8):
        total = total + z_in[j].astype(F32)
    for m in range(2):
        for h in range(2):
            to = 512 * m + 256 * h
            wgrad[:, to : to + 256] = total[8 * h : 8 * h + 8, 256 * m : 256 * m + 256]
    last = pltpu.make_async_copy(wgrad, wgrad_hbm, sem.at[4, 0])
    last.start()

    def ended(i):
        for move in moves(i):
            move.wait()

    loop(8, ended)
    for move in early:
        move.wait()
    last.wait()


def body(inputs, cotangent, w_value, right_factor, left_factor):
    vmem = pl.BlockSpec(memory_space=pltpu.VMEM)
    hbm = pl.BlockSpec(memory_space=pl.ANY)

    def scratch(*shape, dtype=BF16):
        return pltpu.VMEM(shape, dtype)

    def array(*shape, dtype=BF16):
        return jax.ShapeDtypeStruct(shape, dtype)

    square = scratch(1024, 1024)
    wire = scratch(N, 16, 512)
    x2, u2 = inputs.reshape(2, 512, 1024), cotangent.reshape(2, 512, 1024)
    kept = pl.pallas_call(
        mixer,
        name="mixer",
        out_shape=(
            square,
            square,
            wire,
            scratch(1024, 1024, dtype=F32),
            scratch(2, 512, 512),
            scratch(2, 512, 512),
            scratch(4, 256, 256),
            scratch(4, 256, 256),
            scratch(8, 16, 512),
            scratch(2, 512, 512),
            scratch(2, 512, 512),
        ),
        in_specs=[hbm, hbm, vmem, hbm, hbm],
        out_specs=(vmem,) * 11,
        scratch_shapes=[scratch(2, 512, 512), scratch(4, 256, 256)]
        + [wire] * 7
        + [scratch(4, 4, 4, 2, 16, 512)]
        + [square] * 9
        + [scratch(1024, 256)]
        + [scratch(4, 4, 4, 16, 512)] * 3
        + [scratch(4, 16, 512)]
        + [pltpu.SemaphoreType.DMA((n,)) for n in (8, 8, 10, 8, 10, 18)],
        compiler_params=pltpu.CompilerParams(
            collective_id=0, has_side_effects=True, vmem_limit_bytes=46 << 20
        ),
        cost_estimate=pl.CostEstimate(flops=26_000_000_000, bytes_accessed=14_000_000, transcendentals=0),
    )(x2, u2, w_value, right_factor, left_factor)
    kept = [pltpu.with_memory_space_constraint(k, pltpu.VMEM) for k in kept]
    mixed, igrad, rgrad, lgrad, wgrad = pl.pallas_call(
        finish,
        name="finish",
        out_shape=(
            array(2, 512, 1024),
            array(2, 512, 1024),
            array(2, 512, 512, dtype=F32),
            array(4, 256, 256, dtype=F32),
            array(8, 1024, dtype=F32),
        ),
        in_specs=[vmem] * 11,
        out_specs=(hbm,) * 5,
        scratch_shapes=[
            scratch(2, 512, 512),
            scratch(2, 512, 512),
            scratch(2, 512, 512, dtype=F32),
            scratch(4, 256, 256, dtype=F32),
            scratch(8, 1024, dtype=F32),
            pltpu.SemaphoreType.DMA((5, 8)),
        ],
        compiler_params=pltpu.CompilerParams(vmem_limit_bytes=10 << 20),
        cost_estimate=pl.CostEstimate(flops=10_000_000, bytes_accessed=7_000_000, transcendentals=0),
    )(*kept)
    shape = inputs.shape
    return mixed.reshape(shape), igrad.reshape(shape), rgrad, lgrad, wgrad


def solution(mesh):
    placed = (
        P("dp", "seq", None),
        P("dp", "seq", None),
        P("seq", None),
        P("seq", None, None),
        P("seq", None, None),
    )
    return jax.shard_map(
        body,
        mesh=mesh,
        in_specs=placed,
        out_specs=(
            P("dp", "seq", None),
            P("dp", "seq", None),
            P("seq", None, None),
            P("seq", None, None),
            P("seq", None),
        ),
        check_vma=False,
    )
```

```python
import jax
import jax.numpy as jnp
from jax import lax
from jax.experimental import pallas as pl
from jax.experimental.pallas import tpu as pltpu
from jax.sharding import PartitionSpec as P

MESH = pl.DeviceIdType.MESH
F32 = jnp.float32
BF16 = jnp.bfloat16
N = 128
X4, Z4, Y4, C2 = 4, 4, 4, 2


def seq_of(x, z, y, c):
    return ((x * Z4 + z) * Y4 + y) * C2 + c


def dot(a, b, ca=1, cb=0):
    return lax.dot_general(a, b, (((ca,), (cb,)), ((), ())), preferred_element_type=F32)


def pack(x):
    return jnp.concatenate([x[:, :, :256], x[:, :, 256:]], axis=1).astype(BF16)


def unpack(w):
    w = w.astype(F32)
    return jnp.concatenate([w[:, :8, :], w[:, 8:, :]], axis=2)


def low_rows(shape):
    return lax.broadcasted_iota(jnp.int32, shape, 1) < 4


def interleave(t0, t1):
    low = low_rows(t0.shape)
    return jnp.where(low, t0, pltpu.roll(t1, 4, 1)), jnp.where(low, pltpu.roll(t0, 4, 1), t1)


def pairs(w):
    pair = w.reshape(w.shape[0] // 2, 2, *w.shape[1:])
    return pair[:, 0], pair[:, 1]


def zipped(even, odd):
    return jnp.stack([even, odd], axis=1).reshape(2 * even.shape[0], *even.shape[1:])


def swap_middle(x):
    row = lax.broadcasted_iota(jnp.int32, x.shape, 1)
    up, down = pltpu.roll(x, 6, 1), pltpu.roll(x, 2, 1)
    return jnp.where((row == 2) | (row == 3), up, jnp.where((row == 4) | (row == 5), down, x))


def blocks(x):
    e0, o0 = interleave(x[:, :, :128], x[:, :, 128:256])
    e1, o1 = interleave(x[:, :, 256:384], x[:, :, 384:])
    return zipped(jnp.concatenate([e0, e1], axis=1), jnp.concatenate([o0, o1], axis=1)).astype(BF16)


def unblock(w):
    even, odd = pairs(w.astype(F32))
    c0, c1 = interleave(even[:, :8], odd[:, :8])
    c2, c3 = interleave(even[:, 8:], odd[:, 8:])
    return jnp.concatenate([c0, c1, c2, c3], axis=2)


def to_owners(t0, t1):
    return blocks(swap_middle(zipped(*interleave(t0, t1))))


def from_owners(w):
    return interleave(*pairs(swap_middle(unblock(w))))


def loop(count, step):
    def run(i, carry):
        step(i)
        return carry

    lax.fori_loop(0, count, run, 0)


def at(i, size):
    return pl.ds(pl.multiple_of(i * size, size), size)


def results(i, m, x_ref, u_ref, r4, back_ref, mixed, igrad):
    parts = from_owners(r4[at(i, 32), :, 128 * m : 128 * m + 128])
    cols = slice(512 * m, 512 * m + 512)
    for a in range(2):
        rows = pl.ds(pl.multiple_of(512 * a + i * 64, 64), 64)
        second = parts[a].reshape(64, 512)
        mixed[a, at(i, 64), :] = (x_ref[rows, cols].astype(F32) * second).astype(BF16)
        igrad[a, at(i, 64), :] = (u_ref[rows, cols].astype(F32) * second + back_ref[rows, cols]).astype(BF16)


def mixer(
    x_hbm, u_hbm, w_ref, r_hbm, l_hbm,
    x_ref, u_ref, r4, back_ref, rg_own, rg_other, lg_all, z_in, mixed_0, igrad_0,
    r_ref, l_ref, s1, r1, s2, r2, s3, r3, s4,
    wall, wm, m_ref, mt_ref, t_ref, g_ref, f_ref, v_ref, fg_ref, vg_ref,
    lg_mid, core_in, plane_out, plane_in, z_out,
    send_sem, recv_sem, own_sem, w_sem, x_sem, in_sem,
):
    me = lax.axis_index("seq")
    dp = lax.axis_index("dp")
    x = lax.div(me, 32)
    z = lax.rem(lax.div(me, 8), 4)
    y = lax.rem(lax.div(me, 2), 4)
    c = lax.rem(me, 2)

    def remote(src, dst, send, recv, target, group=None):
        return pltpu.make_async_remote_copy(
            src_ref=src, dst_ref=dst, send_sem=send, recv_sem=recv,
            device_id=(dp if group is None else group, target), device_id_type=MESH,
        )

    def settle(ref, sem):
        pltpu.make_async_copy(ref, ref, sem).wait()

    def half(m):
        return pl.ds(128 * m, 128)

    pair_me, line_me = 2 * me + dp, dp * N + me

    def to_owner(i, m, src, dst, q, k):
        remote(
            src.at[2 * q + k, :, half(m)], dst.at[line_me, :, half(m)], send_sem.at[2 * i + m], recv_sem.at[2 * i + m], q, k
        ).start()

    def to_source(i, m, src, dst, q, k):
        remote(
            src.at[k * N + q, :, half(m)], dst.at[pair_me, :, half(m)], send_sem.at[2 * i + m], recv_sem.at[2 * i + m], q, k
        ).start()

    def own(i, m, src, dst):
        mine, there = (line_me, pair_me) if i >= 2 else (pair_me, line_me)
        return pltpu.make_async_copy(src.at[mine, :, half(m)], dst.at[there, :, half(m)], own_sem.at[2 * i + m])

    def exchange(i, m, src, dst):
        own(i, m, src, dst).start()

        def send(k):
            q, group = lax.rem(me + lax.div(k + 1, 2), N), lax.rem(dp + k + 1, 2)
            (to_source if i >= 2 else to_owner)(i, m, src, dst, q, group)

        loop(2 * N - 1, send)

    def arrived(i, m, src, dst):
        own(i, m, src, dst).wait()
        settle(dst.at[pl.ds(0, 2 * N - 1), :, half(m)], recv_sem.at[2 * i + m])

    def sent(i, src):
        for m in range(2):
            settle(src.at[pl.ds(0, 2 * N - 1), :, half(m)], send_sem.at[2 * i + m])

    def piece(j):
        return lax.rem(lax.div(me, 8) + j, 16)

    def load(j):
        b0 = pl.multiple_of(piece(j) * 32, 32)
        for a in range(2):
            for src, dst in ((x_hbm, x_ref), (u_hbm, u_ref)):
                pltpu.make_async_copy(
                    src.at[a, pl.ds(b0, 32)], dst.at[pl.ds(512 * a + b0, 32)], in_sem.at[j]
                ).start()

    loop(16, load)
    left_in = pltpu.make_async_copy(l_hbm, l_ref, in_sem.at[16])
    left_in.start()
    right_in = pltpu.make_async_copy(r_hbm, r_ref, in_sem.at[17])
    right_in.start()

    ready = pltpu.get_barrier_semaphore()

    def greet(group, target):
        pl.semaphore_signal(ready, inc=1, device_id=(group, target), device_id_type=MESH)

    loop(2 * N - 1, lambda k: greet(lax.rem(dp + k + 1, 2), lax.rem(me + lax.div(k + 1, 2), N)))

    def second_grad(j):
        i = piece(j)
        settle(s1.at[pl.ds(0, 32)], in_sem.at[j])
        a0, a1 = at(i, 32), pl.ds(pl.multiple_of(512 + i * 32, 32), 32)
        for m in range(2):
            cols = slice(512 * m, 512 * m + 512)
            t0 = x_ref[a0, cols].astype(F32) * u_ref[a0, cols].astype(F32)
            t1 = x_ref[a1, cols].astype(F32) * u_ref[a1, cols].astype(F32)
            s1[at(i, 16), :, 128 * m : 128 * m + 128] = to_owners(t0.reshape(4, 8, 512), t1.reshape(4, 8, 512))

    def second_grad_out(j):
        def send(k):
            d = 8 * piece(j) + lax.rem(me + lax.div(k, 2), 8)
            group = lax.rem(dp + k, 2)

            @pl.when((d != me) | (group != dp))
            def _():
                to_owner(0, 0, s1, r1, d, group)

        loop(16, send)

    for m in range(2):
        rows = w_ref[:, 512 * m : 512 * m + 512].astype(F32).reshape(1, 8, 512)
        wall[x, z, y, c, :, 256 * m : 256 * m + 256] = pack(rows).reshape(16, 256)

    def spread(phase, block, targets):
        for t in targets:
            remote(block, block, w_sem.at[2 * phase], w_sem.at[2 * phase + 1], t).start()

    def spread_done(phase, like):
        settle(like, w_sem.at[2 * phase + 1])
        settle(like, w_sem.at[2 * phase])


    loop(4, lambda j: second_grad(j))
    pl.semaphore_wait(ready, 2 * N - 1)
    spread(0, wall.at[x, z, y, c], [seq_of(x, lax.rem(z + i, 4), y, c) for i in (1, 2, 3)])

    def ahead(j):
        second_grad_out(j)
        second_grad(j + 4)

    loop(12, ahead)
    loop(4, lambda j: second_grad_out(j + 12))
    own(0, 0, s1, r1).start()
    exchange(0, 1, s1, r1)

    def widen(j):
        row = lax.broadcasted_iota(jnp.int32, (256, 512), 0)
        col = lax.broadcasted_iota(jnp.int32, (256, 512), 1)
        return (col == 2 * row + j).astype(F32).astype(BF16)

    def place(i):
        row = lax.broadcasted_iota(jnp.int32, (256, 512), 0) + i * 256
        col = lax.broadcasted_iota(jnp.int32, (256, 512), 1)
        return (2 * lax.rem(col, 256) + lax.div(col, 256) == row).astype(F32).astype(BF16)

    def build(transposed, out):
        def wide(j):
            t_ref[at(j, 256), :] = dot(l_ref[2 * dp + j], widen(j), ca=0 if transposed else 1).astype(BF16)

        loop(2, wide)

        def rows(i):
            out[at(i, 256), :] = dot(place(i), t_ref[...]).astype(BF16)

        loop(2, rows)

    def unpack_cols(src, dst, m):
        def step(i):
            part = unblock(src[at(i, 32), :, 128 * m : 128 * m + 128])
            dst[at(i, 128), 512 * m : 512 * m + 512] = part.reshape(128, 512).astype(BF16)

        loop(8, step)

    def columns_product(big, cols_ref, out, m):
        def step(s):
            t = dot(big[...], cols_ref[at(s, 512), 512 * m : 512 * m + 512])
            out[at(s, 128), :, 128 * m : 128 * m + 128] = blocks(t.reshape(64, 8, 512))

        loop(2, step)

    def first_grad_columns(m):
        arrived(0, m, s1, r1)
        unpack_cols(r1, g_ref, m)
        columns_product(mt_ref, g_ref, s3, m)
        exchange(2, m, s3, r3)

    def second_columns(m):
        arrived(1, m, s2, r2)
        unpack_cols(r2, f_ref, m)
        columns_product(m_ref, f_ref, s4, m)
        exchange(3, m, s4, r4)

    def first_grad(m):
        arrived(2, m, s3, r3)

        def step(i):
            t0, t1 = from_owners(r3[at(i, 32), :, 128 * m : 128 * m + 128])
            cols = slice(512 * m, 512 * m + 512)
            fg_ref[at(i, 64), cols] = t0.reshape(64, 512).astype(BF16)
            fg_ref[pl.ds(pl.multiple_of(512 + i * 64, 64), 64), cols] = t1.reshape(64, 512).astype(BF16)

        loop(8, step)

    spread_done(0, wall.at[0, pl.ds(0, 3), 0, 0])
    spread(1, wall.at[x, :, y, c], [seq_of(lax.rem(x + i, 4), z, y, c) for i in (1, 2, 3)])
    left_in.wait()
    build(True, mt_ref)
    spread_done(1, wall.at[pl.ds(0, 3), :, 0, 0])
    spread(2, wall.at[:, :, y, c], [seq_of(x, z, lax.rem(y + i, 4), c) for i in (1, 2, 3)])
    first_grad_columns(0)
    spread_done(2, wall.at[:, :, pl.ds(0, 3), 0])
    spread(3, wall.at[:, :, :, c], [seq_of(x, z, y, 1 - c)])
    right_in.wait()
    spread_done(3, wall.at[:, :, :, 0])

    def unpack_weight(i):
        for m in range(2):
            part = wall[i, :, :, :, :, 256 * m : 256 * m + 256].reshape(32, 16, 256)
            wm[at(i, 256), 512 * m : 512 * m + 512] = unpack(part).reshape(256, 512).astype(BF16)

    loop(4, unpack_weight)

    def value(i):
        v_ref[at(i, 256), :] = dot(x_ref[at(i, 256), :], wm[...]).astype(BF16)

    loop(4, value)

    def first(m):
        def step(i):
            cols = slice(512 * m, 512 * m + 512)
            t0 = dot(r_ref[0, at(i, 256), :], v_ref[0:512, cols])
            t1 = dot(r_ref[1, at(i, 256), :], v_ref[512:1024, cols])
            s2[at(i, 128), :, 128 * m : 128 * m + 128] = to_owners(t0.reshape(32, 8, 512), t1.reshape(32, 8, 512))

        loop(2, step)
        exchange(1, m, s2, r2)

    first(0)
    first(1)
    first_grad_columns(1)
    build(False, m_ref)
    first_grad(0)
    second_columns(0)
    second_columns(1)

    def left_all(i):
        rows = dot(g_ref[at(i, 256), :], f_ref[0:512, :], cb=1)
        rows = rows + dot(g_ref[pl.ds(pl.multiple_of(512 + i * 256, 256), 256), :], f_ref[512:1024, :], cb=1)
        row = lax.broadcasted_iota(jnp.int32, (256, 512), 0)
        col = lax.broadcasted_iota(jnp.int32, (256, 512), 1)
        t_ref[at(i, 256), :] = jnp.where(lax.rem(row, 2) == lax.rem(col, 2), rows, 0.0).astype(BF16)

    loop(2, left_all)

    def left_narrow(i):
        row = lax.broadcasted_iota(jnp.int32, (512, 256), 0)
        col = lax.broadcasted_iota(jnp.int32, (512, 256), 1)
        narrow = (lax.div(row, 2) == col).astype(F32).astype(BF16)
        lg_mid[at(i, 256), :] = dot(t_ref[at(i, 256), :], narrow).astype(BF16)

    loop(2, left_narrow)

    def left_place(j):
        row = lax.broadcasted_iota(jnp.int32, (256, 512), 0)
        col = lax.broadcasted_iota(jnp.int32, (256, 512), 1)
        take = (2 * row + j == col).astype(F32).astype(BF16)
        lg_all[2 * dp + j] = dot(take, lg_mid[...]).astype(BF16)

    loop(2, left_place)
    done = lg_all.at[pl.ds(2 * dp, 2)]
    left_swap = remote(done, done, x_sem.at[0], x_sem.at[1], me, 1 - dp)
    left_swap.start()

    first_grad(1)

    def right_part(i):
        rg_own[i] = dot(fg_ref[at(i, 512), :], v_ref[at(i, 512), :], cb=1).astype(BF16)

    loop(2, right_part)
    right_swap = remote(rg_own, rg_other, x_sem.at[2], x_sem.at[3], me, 1 - dp)
    right_swap.start()

    def value_grad(i):
        vg_ref[at(i, 512), :] = dot(r_ref[i], fg_ref[at(i, 512), :], ca=0).astype(BF16)

    loop(2, value_grad)

    def weight_part(i):
        for m in range(2):
            t = dot(x_ref[:, at(i, 256)], vg_ref[:, 512 * m : 512 * m + 512], ca=0)
            wall[i, :, :, :, :, 256 * m : 256 * m + 256] = pack(t.reshape(32, 8, 512)).reshape(4, 4, 2, 16, 256)

    loop(4, weight_part)
    to_core = remote(wall.at[:, :, :, 1 - c], core_in, x_sem.at[4], x_sem.at[5], seq_of(x, z, y, 1 - c))
    to_core.start()

    def back(i):
        back_ref[at(i, 256), :] = dot(vg_ref[at(i, 256), :], wm[...], cb=1)

    loop(2, back)
    to_core.wait()

    def add_core(i):
        mine = wall[i, :, :, c].astype(F32)
        plane_out[i] = (mine + core_in[i].astype(F32)).astype(BF16)

    loop(4, add_core)
    keep = pltpu.make_async_copy(plane_out.at[x, :, y], plane_in.at[x, y], own_sem.at[8])
    keep.start()
    for i in range(1, 16):
        tx, ty = lax.rem(x + i // 4, 4), lax.rem(y + i % 4, 4)
        remote(plane_out.at[tx, :, ty], plane_in.at[x, y], x_sem.at[6], x_sem.at[7], seq_of(tx, z, ty, c)).start()

    loop(2, lambda i: back(i + 2))
    keep.wait()
    settle(s1.at[pl.ds(0, 120)], x_sem.at[7])
    settle(s1.at[pl.ds(0, 120)], x_sem.at[6])

    def add_plane(i):
        total = jnp.zeros((16, 512), F32)
        for j in range(16):
            total = total + plane_in[j // 4, j % 4, i].astype(F32)
        z_out[i] = total.astype(BF16)

    loop(4, add_plane)
    zz = z * 2 + dp
    keep = pltpu.make_async_copy(z_out.at[z], z_in.at[zz], own_sem.at[9])
    keep.start()
    for i in range(1, 8):
        tz = lax.rem(zz + i, 8)
        th = lax.div(tz, 2)
        remote(z_out.at[th], z_in.at[zz], x_sem.at[8], x_sem.at[9], seq_of(x, th, y, c), lax.rem(tz, 2)).start()

    arrived(3, 0, s4, r4)

    def results_0(i):
        results(i, 0, x_ref, u_ref, r4, back_ref, mixed_0, igrad_0)

    loop(8, results_0)

    keep.wait()
    settle(s1.at[pl.ds(0, 14)], x_sem.at[9])
    settle(s1.at[pl.ds(0, 14)], x_sem.at[8])
    sent(0, s1)
    sent(1, s2)
    sent(2, s3)
    left_swap.wait()
    right_swap.wait()
    sent(3, s4)
    arrived(3, 1, s4, r4)


def finish(
    x_ref, u_ref, r4, back_ref, rg_own, rg_other, lg_all, z_in, mixed_0, igrad_0,
    mixed_hbm, igrad_hbm, rgrad_hbm, lgrad_hbm, wgrad_hbm,
    mixed_1, igrad_1, rgrad, lgrad, wgrad, sem,
):
    def moves(i):
        b, q = at(i, 64), at(i, 32)
        return (
            pltpu.make_async_copy(mixed_1.at[:, b], mixed_hbm.at[:, b, pl.ds(512, 512)], sem.at[0, i]),
            pltpu.make_async_copy(igrad_1.at[:, b], igrad_hbm.at[:, b, pl.ds(512, 512)], sem.at[1, i]),
            pltpu.make_async_copy(rgrad.at[:, b], rgrad_hbm.at[:, b], sem.at[2, i]),
            pltpu.make_async_copy(lgrad.at[:, q], lgrad_hbm.at[:, q], sem.at[3, i]),
        )

    early = (
        pltpu.make_async_copy(mixed_0, mixed_hbm.at[:, :, pl.ds(0, 512)], sem.at[4, 1]),
        pltpu.make_async_copy(igrad_0, igrad_hbm.at[:, :, pl.ds(0, 512)], sem.at[4, 2]),
    )
    for move in early:
        move.start()

    def part(i):
        b, q = at(i, 64), at(i, 32)
        for a in range(2):
            rgrad[a, b, :] = rg_own[a, b, :].astype(F32) + rg_other[a, b, :].astype(F32)
        for k in range(4):
            lgrad[k, q, :] = lg_all[k, q, :].astype(F32)
        results(i, 1, x_ref, u_ref, r4, back_ref, mixed_1, igrad_1)
        for move in moves(i):
            move.start()

    loop(8, part)
    total = jnp.zeros((16, 512), F32)
    for j in range(8):
        total = total + z_in[j].astype(F32)
    for m in range(2):
        for h in range(2):
            to = 512 * m + 256 * h
            wgrad[:, to : to + 256] = total[8 * h : 8 * h + 8, 256 * m : 256 * m + 256]
    last = pltpu.make_async_copy(wgrad, wgrad_hbm, sem.at[4, 0])
    last.start()

    def ended(i):
        for move in moves(i):
            move.wait()

    loop(8, ended)
    for move in early:
        move.wait()
    last.wait()


def body(inputs, cotangent, w_value, right_factor, left_factor):
    vmem = pl.BlockSpec(memory_space=pltpu.VMEM)
    hbm = pl.BlockSpec(memory_space=pl.ANY)

    def scratch(*shape, dtype=BF16):
        return pltpu.VMEM(shape, dtype)

    def array(*shape, dtype=BF16):
        return jax.ShapeDtypeStruct(shape, dtype)

    square = scratch(1024, 1024)
    wire = scratch(2 * N, 16, 256)
    x2, u2 = inputs.reshape(2, 512, 1024), cotangent.reshape(2, 512, 1024)
    kept = pl.pallas_call(
        mixer,
        name="mixer",
        out_shape=(
            square,
            square,
            wire,
            scratch(1024, 1024, dtype=F32),
            scratch(2, 512, 512),
            scratch(2, 512, 512),
            scratch(4, 256, 256),
            scratch(8, 16, 512),
            scratch(2, 512, 512),
            scratch(2, 512, 512),
        ),
        in_specs=[hbm, hbm, vmem, hbm, hbm],
        out_specs=(vmem,) * 10,
        scratch_shapes=[scratch(2, 512, 512), scratch(4, 256, 256)]
        + [wire] * 7
        + [scratch(4, 4, 4, 2, 16, 512)]
        + [square]
        + [scratch(512, 512)] * 3
        + [square] * 5
        + [scratch(512, 256)]
        + [scratch(4, 4, 4, 16, 512)] * 3
        + [scratch(4, 16, 512)]
        + [pltpu.SemaphoreType.DMA((n,)) for n in (8, 8, 10, 8, 10, 18)],
        compiler_params=pltpu.CompilerParams(
            collective_id=0, has_side_effects=True, vmem_limit_bytes=46 << 20
        ),
        cost_estimate=pl.CostEstimate(flops=26_000_000_000, bytes_accessed=14_000_000, transcendentals=0),
    )(x2, u2, w_value, right_factor, left_factor)
    kept = [pltpu.with_memory_space_constraint(k, pltpu.VMEM) for k in kept]
    mixed, igrad, rgrad, lgrad, wgrad = pl.pallas_call(
        finish,
        name="finish",
        out_shape=(
            array(2, 512, 1024),
            array(2, 512, 1024),
            array(2, 512, 512, dtype=F32),
            array(4, 256, 256, dtype=F32),
            array(8, 1024, dtype=F32),
        ),
        in_specs=[vmem] * 10,
        out_specs=(hbm,) * 5,
        scratch_shapes=[
            scratch(2, 512, 512),
            scratch(2, 512, 512),
            scratch(2, 512, 512, dtype=F32),
            scratch(4, 256, 256, dtype=F32),
            scratch(8, 1024, dtype=F32),
            pltpu.SemaphoreType.DMA((5, 8)),
        ],
        compiler_params=pltpu.CompilerParams(vmem_limit_bytes=10 << 20),
        cost_estimate=pl.CostEstimate(flops=10_000_000, bytes_accessed=7_000_000, transcendentals=0),
    )(*kept)
    shape = inputs.shape
    return mixed.reshape(shape), igrad.reshape(shape), rgrad, lgrad, wgrad


def solution(mesh):
    placed = (
        P("dp", "seq", None),
        P("dp", "seq", None),
        P("seq", None),
        P("seq", None, None),
        P("seq", None, None),
    )
    return jax.shard_map(
        body,
        mesh=mesh,
        in_specs=placed,
        out_specs=(
            P("dp", "seq", None),
            P("dp", "seq", None),
            P("seq", None, None),
            P("seq", None, None),
            P("seq", None),
        ),
        check_vma=False,
    )
```

```python
import jax
import jax.numpy as jnp
from jax import lax
from jax.experimental import pallas as pl
from jax.experimental.pallas import tpu as pltpu
from jax.sharding import PartitionSpec as P

MESH = pl.DeviceIdType.MESH
F32 = jnp.float32
BF16 = jnp.bfloat16
N = 128
X4, Z4, Y4, C2 = 4, 4, 4, 2


def seq_of(x, z, y, c):
    return ((x * Z4 + z) * Y4 + y) * C2 + c


def dot(a, b, ca=1, cb=0):
    return lax.dot_general(a, b, (((ca,), (cb,)), ((), ())), preferred_element_type=F32)


def pack(x):
    return jnp.concatenate([x[:, :, :256], x[:, :, 256:]], axis=1).astype(BF16)


def unpack(w):
    w = w.astype(F32)
    return jnp.concatenate([w[:, :8, :], w[:, 8:, :]], axis=2)


def low_rows(shape):
    return lax.broadcasted_iota(jnp.int32, shape, 1) < 4


def interleave(t0, t1):
    low = low_rows(t0.shape)
    return jnp.where(low, t0, pltpu.roll(t1, 4, 1)), jnp.where(low, pltpu.roll(t0, 4, 1), t1)


def pairs(w):
    pair = w.reshape(w.shape[0] // 2, 2, *w.shape[1:])
    return pair[:, 0], pair[:, 1]


def zipped(even, odd):
    return jnp.stack([even, odd], axis=1).reshape(2 * even.shape[0], *even.shape[1:])


def swap_middle(x):
    row = lax.broadcasted_iota(jnp.int32, x.shape, 1)
    up, down = pltpu.roll(x, 6, 1), pltpu.roll(x, 2, 1)
    return jnp.where((row == 2) | (row == 3), up, jnp.where((row == 4) | (row == 5), down, x))


def blocks(x):
    e0, o0 = interleave(x[:, :, :128], x[:, :, 128:256])
    e1, o1 = interleave(x[:, :, 256:384], x[:, :, 384:])
    return zipped(jnp.concatenate([e0, e1], axis=1), jnp.concatenate([o0, o1], axis=1)).astype(BF16)


def unblock(w):
    even, odd = pairs(w.astype(F32))
    c0, c1 = interleave(even[:, :8], odd[:, :8])
    c2, c3 = interleave(even[:, 8:], odd[:, 8:])
    return jnp.concatenate([c0, c1, c2, c3], axis=2)


def to_owners(t0, t1):
    return blocks(swap_middle(zipped(*interleave(t0, t1))))


def from_owners(w):
    return interleave(*pairs(swap_middle(unblock(w))))


def loop(count, step):
    def run(i, carry):
        step(i)
        return carry

    lax.fori_loop(0, count, run, 0)


def at(i, size):
    return pl.ds(pl.multiple_of(i * size, size), size)


def results(i, m, x_ref, u_ref, r4, back_ref, mixed, igrad):
    parts = from_owners(r4[at(i, 32), :, 128 * m : 128 * m + 128])
    cols = slice(512 * m, 512 * m + 512)
    for a in range(2):
        rows = pl.ds(pl.multiple_of(512 * a + i * 64, 64), 64)
        second = parts[a].reshape(64, 512)
        mixed[a, at(i, 64), :] = (x_ref[rows, cols].astype(F32) * second).astype(BF16)
        igrad[a, at(i, 64), :] = (u_ref[rows, cols].astype(F32) * second + back_ref[rows, cols]).astype(BF16)


def mixer(
    x_hbm, u_hbm, w_ref, r_hbm, l_hbm,
    x_ref, u_ref, r4, back_ref, rg_own, rg_other, lg_all, z_in, mixed_0, igrad_0,
    r_ref, l_ref, s1, r1, s2, r2, s3, r3, s4,
    wall, wm, m_ref, mt_ref, t_ref, g_ref, f_ref, v_ref, fg_ref, vg_ref,
    lg_mid, core_in, plane_out, plane_in, z_out,
    send_sem, recv_sem, own_sem, w_sem, x_sem, in_sem,
):
    me = lax.axis_index("seq")
    dp = lax.axis_index("dp")
    x = lax.div(me, 32)
    z = lax.rem(lax.div(me, 8), 4)
    y = lax.rem(lax.div(me, 2), 4)
    c = lax.rem(me, 2)

    def remote(src, dst, send, recv, target, group=None):
        return pltpu.make_async_remote_copy(
            src_ref=src, dst_ref=dst, send_sem=send, recv_sem=recv,
            device_id=(dp if group is None else group, target), device_id_type=MESH,
        )

    def settle(ref, sem):
        pltpu.make_async_copy(ref, ref, sem).wait()

    def half(m):
        return pl.ds(128 * m, 128)

    pair_me, line_me = 2 * me + dp, dp * N + me

    def to_owner(i, m, src, dst, q, k):
        remote(
            src.at[2 * q + k, :, half(m)], dst.at[line_me, :, half(m)], send_sem.at[2 * i + m], recv_sem.at[2 * i + m], q, k
        ).start()

    def to_source(i, m, src, dst, q, k):
        remote(
            src.at[k * N + q, :, half(m)], dst.at[pair_me, :, half(m)], send_sem.at[2 * i + m], recv_sem.at[2 * i + m], q, k
        ).start()

    def own(i, m, src, dst):
        mine, there = (line_me, pair_me) if i >= 2 else (pair_me, line_me)
        return pltpu.make_async_copy(src.at[mine, :, half(m)], dst.at[there, :, half(m)], own_sem.at[2 * i + m])

    def exchange(i, m, src, dst):
        own(i, m, src, dst).start()

        give = to_source if i >= 2 else to_owner

        def send(k):
            q = lax.rem(me + k + 1, N)
            give(i, m, src, dst, q, dp)
            give(i, m, src, dst, q, 1 - dp)

        loop(N - 1, send)
        give(i, m, src, dst, me, 1 - dp)

    def arrived(i, m, src, dst):
        own(i, m, src, dst).wait()
        settle(dst.at[pl.ds(0, 2 * N - 1), :, half(m)], recv_sem.at[2 * i + m])

    def sent(i, src):
        for m in range(2):
            settle(src.at[pl.ds(0, 2 * N - 1), :, half(m)], send_sem.at[2 * i + m])

    def piece(j):
        return lax.rem(lax.div(me, 8) + j, 16)

    def load(j):
        b0 = pl.multiple_of(piece(j) * 32, 32)
        for a in range(2):
            for src, dst in ((x_hbm, x_ref), (u_hbm, u_ref)):
                pltpu.make_async_copy(
                    src.at[a, pl.ds(b0, 32)], dst.at[pl.ds(512 * a + b0, 32)], in_sem.at[j]
                ).start()

    loop(4, load)

    ready = pltpu.get_barrier_semaphore()

    def greet(group, target):
        pl.semaphore_signal(ready, inc=1, device_id=(group, target), device_id_type=MESH)

    def greet_both(k):
        q = lax.rem(me + k + 1, N)
        greet(dp, q)
        greet(1 - dp, q)

    loop(N - 1, greet_both)
    greet(1 - dp, me)
    loop(12, lambda j: load(j + 4))
    left_in = pltpu.make_async_copy(l_hbm, l_ref, in_sem.at[16])
    left_in.start()
    right_in = pltpu.make_async_copy(r_hbm, r_ref, in_sem.at[17])
    right_in.start()

    def second_grad(j):
        i = piece(j)
        settle(s1.at[pl.ds(0, 32)], in_sem.at[j])
        a0, a1 = at(i, 32), pl.ds(pl.multiple_of(512 + i * 32, 32), 32)
        for m in range(2):
            cols = slice(512 * m, 512 * m + 512)
            t0 = x_ref[a0, cols].astype(F32) * u_ref[a0, cols].astype(F32)
            t1 = x_ref[a1, cols].astype(F32) * u_ref[a1, cols].astype(F32)
            s1[at(i, 16), :, 128 * m : 128 * m + 128] = to_owners(t0.reshape(4, 8, 512), t1.reshape(4, 8, 512))

    def second_grad_out(j):
        def send(k):
            d = 8 * piece(j) + lax.rem(me + k, 8)

            @pl.when(d != me)
            def _():
                to_owner(0, 0, s1, r1, d, dp)

            to_owner(0, 0, s1, r1, d, 1 - dp)

        loop(8, send)

    for m in range(2):
        rows = w_ref[:, 512 * m : 512 * m + 512].astype(F32).reshape(1, 8, 512)
        wall[x, z, y, c, :, 256 * m : 256 * m + 256] = pack(rows).reshape(16, 256)

    def spread(phase, block, targets):
        for t in targets:
            remote(block, block, w_sem.at[2 * phase], w_sem.at[2 * phase + 1], t).start()

    def spread_done(phase, like):
        settle(like, w_sem.at[2 * phase + 1])
        settle(like, w_sem.at[2 * phase])


    loop(4, lambda j: second_grad(j))
    pl.semaphore_wait(ready, 2 * N - 1)
    spread(0, wall.at[x, z, y, c], [seq_of(x, lax.rem(z + i, 4), y, c) for i in (1, 2, 3)])

    def ahead(j):
        second_grad_out(j)
        second_grad(j + 4)

    loop(12, ahead)
    loop(4, lambda j: second_grad_out(j + 12))
    own(0, 0, s1, r1).start()
    exchange(0, 1, s1, r1)

    def widen(j):
        row = lax.broadcasted_iota(jnp.int32, (256, 512), 0)
        col = lax.broadcasted_iota(jnp.int32, (256, 512), 1)
        return (col == 2 * row + j).astype(F32).astype(BF16)

    def place(i):
        row = lax.broadcasted_iota(jnp.int32, (256, 512), 0) + i * 256
        col = lax.broadcasted_iota(jnp.int32, (256, 512), 1)
        return (2 * lax.rem(col, 256) + lax.div(col, 256) == row).astype(F32).astype(BF16)

    def build(transposed, out):
        def wide(j):
            t_ref[at(j, 256), :] = dot(l_ref[2 * dp + j], widen(j), ca=0 if transposed else 1).astype(BF16)

        loop(2, wide)

        def rows(i):
            out[at(i, 256), :] = dot(place(i), t_ref[...]).astype(BF16)

        loop(2, rows)

    def unpack_cols(src, dst, m):
        def step(i):
            part = unblock(src[at(i, 32), :, 128 * m : 128 * m + 128])
            dst[at(i, 128), 512 * m : 512 * m + 512] = part.reshape(128, 512).astype(BF16)

        loop(8, step)

    def columns_product(big, cols_ref, out, m):
        def step(s):
            t = dot(big[...], cols_ref[at(s, 512), 512 * m : 512 * m + 512])
            out[at(s, 128), :, 128 * m : 128 * m + 128] = blocks(t.reshape(64, 8, 512))

        loop(2, step)

    def first_grad_columns(m):
        arrived(0, m, s1, r1)
        unpack_cols(r1, g_ref, m)
        columns_product(mt_ref, g_ref, s3, m)
        exchange(2, m, s3, r3)

    def second_columns(m):
        arrived(1, m, s2, r2)
        unpack_cols(r2, f_ref, m)
        columns_product(m_ref, f_ref, s4, m)
        exchange(3, m, s4, r4)

    def first_grad(m):
        arrived(2, m, s3, r3)

        def step(i):
            t0, t1 = from_owners(r3[at(i, 32), :, 128 * m : 128 * m + 128])
            cols = slice(512 * m, 512 * m + 512)
            fg_ref[at(i, 64), cols] = t0.reshape(64, 512).astype(BF16)
            fg_ref[pl.ds(pl.multiple_of(512 + i * 64, 64), 64), cols] = t1.reshape(64, 512).astype(BF16)

        loop(8, step)

    spread_done(0, wall.at[0, pl.ds(0, 3), 0, 0])
    spread(1, wall.at[x, :, y, c], [seq_of(lax.rem(x + i, 4), z, y, c) for i in (1, 2, 3)])
    left_in.wait()
    build(True, mt_ref)
    spread_done(1, wall.at[pl.ds(0, 3), :, 0, 0])
    spread(2, wall.at[:, :, y, c], [seq_of(x, z, lax.rem(y + i, 4), c) for i in (1, 2, 3)])
    first_grad_columns(0)
    spread_done(2, wall.at[:, :, pl.ds(0, 3), 0])
    spread(3, wall.at[:, :, :, c], [seq_of(x, z, y, 1 - c)])
    right_in.wait()
    spread_done(3, wall.at[:, :, :, 0])

    def unpack_weight(i):
        for m in range(2):
            part = wall[i, :, :, :, :, 256 * m : 256 * m + 256].reshape(32, 16, 256)
            wm[at(i, 256), 512 * m : 512 * m + 512] = unpack(part).reshape(256, 512).astype(BF16)

    loop(4, unpack_weight)

    def value(i):
        v_ref[at(i, 256), :] = dot(x_ref[at(i, 256), :], wm[...]).astype(BF16)

    loop(4, value)

    def first(m):
        def step(i):
            cols = slice(512 * m, 512 * m + 512)
            t0 = dot(r_ref[0, at(i, 256), :], v_ref[0:512, cols])
            t1 = dot(r_ref[1, at(i, 256), :], v_ref[512:1024, cols])
            s2[at(i, 128), :, 128 * m : 128 * m + 128] = to_owners(t0.reshape(32, 8, 512), t1.reshape(32, 8, 512))

        loop(2, step)
        exchange(1, m, s2, r2)

    first(0)
    first(1)
    first_grad_columns(1)
    build(False, m_ref)
    first_grad(0)
    second_columns(0)
    second_columns(1)

    def left_all(i):
        rows = dot(g_ref[at(i, 256), :], f_ref[0:512, :], cb=1)
        rows = rows + dot(g_ref[pl.ds(pl.multiple_of(512 + i * 256, 256), 256), :], f_ref[512:1024, :], cb=1)
        row = lax.broadcasted_iota(jnp.int32, (256, 512), 0)
        col = lax.broadcasted_iota(jnp.int32, (256, 512), 1)
        t_ref[at(i, 256), :] = jnp.where(lax.rem(row, 2) == lax.rem(col, 2), rows, 0.0).astype(BF16)

    loop(2, left_all)

    def left_narrow(i):
        row = lax.broadcasted_iota(jnp.int32, (512, 256), 0)
        col = lax.broadcasted_iota(jnp.int32, (512, 256), 1)
        narrow = (lax.div(row, 2) == col).astype(F32).astype(BF16)
        lg_mid[at(i, 256), :] = dot(t_ref[at(i, 256), :], narrow).astype(BF16)

    loop(2, left_narrow)

    def left_place(j):
        row = lax.broadcasted_iota(jnp.int32, (256, 512), 0)
        col = lax.broadcasted_iota(jnp.int32, (256, 512), 1)
        take = (2 * row + j == col).astype(F32).astype(BF16)
        lg_all[2 * dp + j] = dot(take, lg_mid[...]).astype(BF16)

    loop(2, left_place)
    done = lg_all.at[pl.ds(2 * dp, 2)]
    left_swap = remote(done, done, x_sem.at[0], x_sem.at[1], me, 1 - dp)
    left_swap.start()

    first_grad(1)

    def right_part(i):
        rg_own[i] = dot(fg_ref[at(i, 512), :], v_ref[at(i, 512), :], cb=1).astype(BF16)

    loop(2, right_part)
    right_swap = remote(rg_own, rg_other, x_sem.at[2], x_sem.at[3], me, 1 - dp)
    right_swap.start()

    def value_grad(i):
        vg_ref[at(i, 512), :] = dot(r_ref[i], fg_ref[at(i, 512), :], ca=0).astype(BF16)

    loop(2, value_grad)

    def weight_part(i):
        for m in range(2):
            t = dot(x_ref[:, at(i, 256)], vg_ref[:, 512 * m : 512 * m + 512], ca=0)
            wall[i, :, :, :, :, 256 * m : 256 * m + 256] = pack(t.reshape(32, 8, 512)).reshape(4, 4, 2, 16, 256)

    loop(4, weight_part)
    to_core = remote(wall.at[:, :, :, 1 - c], core_in, x_sem.at[4], x_sem.at[5], seq_of(x, z, y, 1 - c))
    to_core.start()

    def back(i):
        back_ref[at(i, 256), :] = dot(vg_ref[at(i, 256), :], wm[...], cb=1)

    loop(2, back)
    to_core.wait()

    def add_core(i):
        mine = wall[i, :, :, c].astype(F32)
        plane_out[i] = (mine + core_in[i].astype(F32)).astype(BF16)

    loop(4, add_core)
    keep = pltpu.make_async_copy(plane_out.at[x, :, y], plane_in.at[x, y], own_sem.at[8])
    keep.start()
    for i in range(1, 16):
        tx, ty = lax.rem(x + i // 4, 4), lax.rem(y + i % 4, 4)
        remote(plane_out.at[tx, :, ty], plane_in.at[x, y], x_sem.at[6], x_sem.at[7], seq_of(tx, z, ty, c)).start()

    loop(2, lambda i: back(i + 2))
    keep.wait()
    settle(s1.at[pl.ds(0, 120)], x_sem.at[7])
    settle(s1.at[pl.ds(0, 120)], x_sem.at[6])

    def add_plane(i):
        total = jnp.zeros((16, 512), F32)
        for j in range(16):
            total = total + plane_in[j // 4, j % 4, i].astype(F32)
        z_out[i] = total.astype(BF16)

    loop(4, add_plane)
    zz = z * 2 + dp
    keep = pltpu.make_async_copy(z_out.at[z], z_in.at[zz], own_sem.at[9])
    keep.start()
    for i in range(1, 8):
        tz = lax.rem(zz + i, 8)
        th = lax.div(tz, 2)
        remote(z_out.at[th], z_in.at[zz], x_sem.at[8], x_sem.at[9], seq_of(x, th, y, c), lax.rem(tz, 2)).start()

    arrived(3, 0, s4, r4)

    def results_0(i):
        results(i, 0, x_ref, u_ref, r4, back_ref, mixed_0, igrad_0)

    loop(8, results_0)

    keep.wait()
    settle(s1.at[pl.ds(0, 14)], x_sem.at[9])
    settle(s1.at[pl.ds(0, 14)], x_sem.at[8])
    sent(0, s1)
    sent(1, s2)
    sent(2, s3)
    left_swap.wait()
    right_swap.wait()
    sent(3, s4)
    arrived(3, 1, s4, r4)


def finish(
    x_ref, u_ref, r4, back_ref, rg_own, rg_other, lg_all, z_in, mixed_0, igrad_0,
    mixed_hbm, igrad_hbm, rgrad_hbm, lgrad_hbm, wgrad_hbm,
    mixed_1, igrad_1, rgrad, lgrad, wgrad, sem,
):
    def moves(i):
        b, q = at(i, 64), at(i, 32)
        return (
            pltpu.make_async_copy(mixed_1.at[:, b], mixed_hbm.at[:, b, pl.ds(512, 512)], sem.at[0, i]),
            pltpu.make_async_copy(igrad_1.at[:, b], igrad_hbm.at[:, b, pl.ds(512, 512)], sem.at[1, i]),
            pltpu.make_async_copy(rgrad.at[:, b], rgrad_hbm.at[:, b], sem.at[2, i]),
            pltpu.make_async_copy(lgrad.at[:, q], lgrad_hbm.at[:, q], sem.at[3, i]),
        )

    early = (
        pltpu.make_async_copy(mixed_0, mixed_hbm.at[:, :, pl.ds(0, 512)], sem.at[4, 1]),
        pltpu.make_async_copy(igrad_0, igrad_hbm.at[:, :, pl.ds(0, 512)], sem.at[4, 2]),
    )
    for move in early:
        move.start()

    def part(i):
        b, q = at(i, 64), at(i, 32)
        for a in range(2):
            rgrad[a, b, :] = rg_own[a, b, :].astype(F32) + rg_other[a, b, :].astype(F32)
        for k in range(4):
            lgrad[k, q, :] = lg_all[k, q, :].astype(F32)
        results(i, 1, x_ref, u_ref, r4, back_ref, mixed_1, igrad_1)
        for move in moves(i):
            move.start()

    loop(8, part)
    total = jnp.zeros((16, 512), F32)
    for j in range(8):
        total = total + z_in[j].astype(F32)
    for m in range(2):
        for h in range(2):
            to = 512 * m + 256 * h
            wgrad[:, to : to + 256] = total[8 * h : 8 * h + 8, 256 * m : 256 * m + 256]
    last = pltpu.make_async_copy(wgrad, wgrad_hbm, sem.at[4, 0])
    last.start()

    def ended(i):
        for move in moves(i):
            move.wait()

    loop(8, ended)
    for move in early:
        move.wait()
    last.wait()


def body(inputs, cotangent, w_value, right_factor, left_factor):
    vmem = pl.BlockSpec(memory_space=pltpu.VMEM)
    hbm = pl.BlockSpec(memory_space=pl.ANY)

    def scratch(*shape, dtype=BF16):
        return pltpu.VMEM(shape, dtype)

    def array(*shape, dtype=BF16):
        return jax.ShapeDtypeStruct(shape, dtype)

    square = scratch(1024, 1024)
    wire = scratch(2 * N, 16, 256)
    x2, u2 = inputs.reshape(2, 512, 1024), cotangent.reshape(2, 512, 1024)
    kept = pl.pallas_call(
        mixer,
        name="mixer",
        out_shape=(
            square,
            square,
            wire,
            scratch(1024, 1024, dtype=F32),
            scratch(2, 512, 512),
            scratch(2, 512, 512),
            scratch(4, 256, 256),
            scratch(8, 16, 512),
            scratch(2, 512, 512),
            scratch(2, 512, 512),
        ),
        in_specs=[hbm, hbm, vmem, hbm, hbm],
        out_specs=(vmem,) * 10,
        scratch_shapes=[scratch(2, 512, 512), scratch(4, 256, 256)]
        + [wire] * 7
        + [scratch(4, 4, 4, 2, 16, 512)]
        + [square]
        + [scratch(512, 512)] * 3
        + [square] * 5
        + [scratch(512, 256)]
        + [scratch(4, 4, 4, 16, 512)] * 3
        + [scratch(4, 16, 512)]
        + [pltpu.SemaphoreType.DMA((n,)) for n in (8, 8, 10, 8, 10, 18)],
        compiler_params=pltpu.CompilerParams(
            collective_id=0, has_side_effects=True, vmem_limit_bytes=46 << 20
        ),
        cost_estimate=pl.CostEstimate(flops=26_000_000_000, bytes_accessed=14_000_000, transcendentals=0),
    )(x2, u2, w_value, right_factor, left_factor)
    kept = [pltpu.with_memory_space_constraint(k, pltpu.VMEM) for k in kept]
    mixed, igrad, rgrad, lgrad, wgrad = pl.pallas_call(
        finish,
        name="finish",
        out_shape=(
            array(2, 512, 1024),
            array(2, 512, 1024),
            array(2, 512, 512, dtype=F32),
            array(4, 256, 256, dtype=F32),
            array(8, 1024, dtype=F32),
        ),
        in_specs=[vmem] * 10,
        out_specs=(hbm,) * 5,
        scratch_shapes=[
            scratch(2, 512, 512),
            scratch(2, 512, 512),
            scratch(2, 512, 512, dtype=F32),
            scratch(4, 256, 256, dtype=F32),
            scratch(8, 1024, dtype=F32),
            pltpu.SemaphoreType.DMA((5, 8)),
        ],
        compiler_params=pltpu.CompilerParams(vmem_limit_bytes=10 << 20),
        cost_estimate=pl.CostEstimate(flops=10_000_000, bytes_accessed=7_000_000, transcendentals=0),
    )(*kept)
    shape = inputs.shape
    return mixed.reshape(shape), igrad.reshape(shape), rgrad, lgrad, wgrad


def solution(mesh):
    placed = (
        P("dp", "seq", None),
        P("dp", "seq", None),
        P("seq", None),
        P("seq", None, None),
        P("seq", None, None),
    )
    return jax.shard_map(
        body,
        mesh=mesh,
        in_specs=placed,
        out_specs=(
            P("dp", "seq", None),
            P("dp", "seq", None),
            P("seq", None, None),
            P("seq", None, None),
            P("seq", None),
        ),
        check_vma=False,
    )
```
